32 devices in a mesh: fsdp: 8 (over y, x, core), rep: 4 (over z).
Axes of the slice: x: 2, y: 2, z: 4, core: 2. Of those that a mesh axis runs over, the one named last changes fastest.
Arguments:
- tokens: bfloat16 [4, 1024, 2048], P('rep', 'fsdp'), may hold values from -6 to 6
- upstream: bfloat16 [4, 7168, 1024], P('rep', 'fsdp'), may hold values from -0.5 to 0.5
- weight: bfloat16 [2, 7168, 2048], P(None, 'fsdp'), may hold values from -0.125 to 0.125
- feedback: float32 [4, 2, 7168, 2048], P('rep', None, 'fsdp'), may hold values from -6 to 6
- momentum: float32 [2, 7168, 2048], P(None, 'fsdp', 'rep'), may hold values from -6 to 6
- right_factor: float32 [2, 7168, 64], P(None, 'fsdp'), may hold values from -6 to 6
Outputs:
- feedback_next: float32 [4, 2, 7168, 2048], P('rep', None, 'fsdp')
- momentum_next: float32 [2, 7168, 2048], P(None, 'fsdp', 'rep')
- weight_next: bfloat16 [2, 7168, 2048], P(None, 'fsdp', 'rep')
- right_next: float32 [2, 7168, 64], P(None, 'fsdp')
The draws below stay inside these ranges and needn't reach their ends.
All inputs are finite; a program needn't handle non-finite values.
Results may differ from the reference program's by a relative error of at most 0.0023.
Values may be sent and summed in bfloat16 or wider, within the bound.
No kernel may reach another device: no remote copies, remote signals or barrier semaphores. Data moves between devices by JAX's collectives and lax.ppermute only.
A program may use at most 128 MiB of HBM per device.

```python
import jax
import jax.numpy as jnp
from jax import lax

D = 2048
FF = 7168
R = 64
TOKENS = 1024
REPLICAS = 4


def shard_levels(stream_key, dims, pieces, least, largest):
    def one(dim, parts):
        heights = jax.random.uniform(jax.random.fold_in(jax.random.fold_in(stream_key, 6), dim), (parts,), jnp.float32, least / len(pieces), largest / len(pieces))
        return jnp.repeat(jnp.exp(heights), dims[dim] // parts).reshape((-1,) + (1,) * (len(dims) - dim - 1))

    level = one(*pieces[0])
    for cut in pieces[1:]:
        level = level * one(*cut)
    return level


def gaussian(rng, shape, spread, reach, pieces=(), kind=jnp.bfloat16):
    loudness = shard_levels(rng, shape, pieces, -0.22, 0.18) if pieces else 1.0
    entries = jax.random.normal(rng, shape, jnp.float32) * spread * loudness
    return jnp.minimum(jnp.maximum(entries, -reach), reach).astype(kind)


def setup_inputs(seed: int = 0) -> dict:
    keys = jax.random.split(jax.random.key(seed), 7)
    return {
        "tokens": gaussian(keys[0], (REPLICAS, TOKENS, D), 1.0, 6.0, ((0, 4), (1, 8))),
        "upstream": gaussian(keys[1], (REPLICAS, FF, TOKENS), (TOKENS ** -0.5), 0.5, ((0, 4), (1, 8))),
        "weight": gaussian(keys[2], (2, FF, D), D ** -0.5, 0.125, ((1, 8),)),
        "feedback": gaussian(keys[3], (REPLICAS, 2, FF, D), 1.0, 6.0, ((0, 4), (2, 8)), jnp.float32),
        "momentum": gaussian(keys[4], (2, FF, D), 1.0, 6.0, ((1, 8), (2, 4)), jnp.float32),
        "right_factor": gaussian(keys[5], (2, FF, R), 1.0, 6.0, ((1, 8),), jnp.float32),
    }


momentum_decay = 0.9
step_rate = 0.05
highest = lax.Precision.HIGHEST

def silu_pair(gate_pre):
    sigmoid = jax.nn.sigmoid(gate_pre)
    return (gate_pre * sigmoid, sigmoid * (1.0 + gate_pre * (1.0 - sigmoid)))

def orthonormal(factor):
    gram_matrix = jnp.einsum('kdr,kds->krs', factor, factor, precision=highest)
    lower_factor = jnp.linalg.cholesky(gram_matrix)
    return lax.linalg.triangular_solve(lower_factor, factor, left_side=False, lower=True, transpose_a=True)

def reference(tokens, upstream, weight, feedback, momentum, right_factor):
    contract_last = (((1,), (1,)), ((), ()))

    def replica_delta(operands):
        rows_in, cotangent, residue = operands
        gate_pre = lax.dot_general(weight[0].astype(jnp.float32), rows_in.astype(jnp.float32), contract_last, preferred_element_type=jnp.float32)
        up_pre = lax.dot_general(weight[1].astype(jnp.float32), rows_in.astype(jnp.float32), contract_last, preferred_element_type=jnp.float32)
        activated, derivative = silu_pair(gate_pre)
        cotangent_wide = cotangent.astype(jnp.float32)
        grad_gate = (cotangent_wide * up_pre * derivative).astype(jnp.bfloat16)
        grad_up = (cotangent_wide * activated).astype(jnp.bfloat16)
        delta_gate = jnp.dot(grad_gate.astype(jnp.float32), rows_in.astype(jnp.float32), preferred_element_type=jnp.float32) + residue[0]
        delta_up = jnp.dot(grad_up.astype(jnp.float32), rows_in.astype(jnp.float32), preferred_element_type=jnp.float32) + residue[1]
        delta = jnp.stack([delta_gate, delta_up])
        left_part = jnp.einsum('kfd,kfr->kdr', delta, right_factor, precision=highest)
        return (delta, left_part)
    delta, left_parts = lax.map(replica_delta, (tokens, upstream, feedback))
    left_mean = jnp.mean(left_parts, axis=0)
    basis = orthonormal(left_mean)

    def right_part(single):
        return jnp.einsum('kfd,kdr->kfr', single, basis, precision=highest)
    right_next = jnp.mean(lax.map(right_part, delta), axis=0)
    approx = jnp.einsum('kdr,kfr->kfd', basis, right_next, precision=highest)
    feedback_next = delta - approx[None]
    momentum_next = momentum_decay * momentum + approx
    weight_next = (weight.astype(jnp.float32) - step_rate * momentum_next).astype(jnp.bfloat16)
    return (feedback_next, momentum_next, weight_next, right_next)
```

```python
import functools

import jax
import jax.numpy as jnp
from jax import lax
from jax.experimental import pallas as pl
from jax.experimental.pallas import tpu as pltpu
from jax.sharding import PartitionSpec as P

momentum_decay = 0.9
step_rate = 0.05
highest = lax.Precision.HIGHEST
f32 = jnp.float32
bf16 = jnp.bfloat16
contract_last = (((1,), (1,)), ((), ()))
MIB = 1024 * 1024


def split2(x):
    hi = x.astype(bf16)
    return hi, (x - hi.astype(f32)).astype(bf16)


def dot(a, b):
    return jnp.dot(a, b, preferred_element_type=f32)


def dot_nt(a, b):
    return lax.dot_general(a, b, contract_last, preferred_element_type=f32)


def params(mib, grid_dims):
    return pltpu.CompilerParams(
        vmem_limit_bytes=mib * MIB, dimension_semantics=("arbitrary",) * grid_dims
    )


def cost(macs, nbytes):
    return pl.CostEstimate(flops=2 * macs, bytes_accessed=nbytes, transcendentals=0)


def feedback_left(feedback, right_t, block=512):
    _, rows, feats = feedback.shape
    rank = right_t.shape[1]

    def body(fb_ref, r_ref, out_ref):
        fb_hi, fb_lo = split2(fb_ref[0])
        r_hi, r_lo = split2(r_ref[0])
        both = dot(jnp.concatenate([r_hi, r_lo], 0), fb_hi)
        out_ref[0] = both[:rank] + both[rank:] + dot(r_hi, fb_lo)

    return pl.pallas_call(
        body,
        grid=(2, feats // block),
        in_specs=[
            pl.BlockSpec((1, rows, block), lambda k, d: (k, 0, d)),
            pl.BlockSpec((1, rank, rows), lambda k, d: (k, 0, 0)),
        ],
        out_specs=pl.BlockSpec((1, rank, block), lambda k, d: (k, 0, d)),
        out_shape=jax.ShapeDtypeStruct((2, rank, feats), f32),
        compiler_params=params(32, 2),
        cost_estimate=cost(2 * rows * feats * 256, 4 * feedback.size),
        name="feedback_left",
    )(feedback, right_t)


def forward_chunk(ids, shards, weight, upstream, right_t, left_in, block):
    count = len(shards)
    per, feats = shards[0].shape
    rows = weight.shape[1]
    rank = right_t.shape[1]
    width = count * per
    steps = rows // block

    def body(ids_ref, *refs):
        tok_refs = refs[:count]
        up_refs = refs[count : 2 * count]
        w_ref, r_ref, left_ref, grad_ref, tok_out, left_out = refs[2 * count :]
        i = pl.program_id(0)

        @pl.when(i == 0)
        def _():
            for j, t in enumerate(tok_refs):
                tok_out[j * per : (j + 1) * per, :] = t[...]

        tok = tok_out[...]
        gate_pre = dot_nt(w_ref[0], tok)
        up_pre = dot_nt(w_ref[1], tok)
        cot = jnp.concatenate([u[...] for u in up_refs], 1).astype(f32)
        s = jax.nn.sigmoid(gate_pre)
        cot_s = cot * s
        span = pl.ds(pl.multiple_of(i * block, block), block)
        grad_ref[0, span, :] = (cot_s * up_pre * (1.0 + gate_pre * (1.0 - s))).astype(bf16)
        grad_ref[1, span, :] = (cot_s * gate_pre).astype(bf16)

        @pl.when(i == steps - 1)
        def _():
            for k in range(2):
                r_hi, r_lo = split2(r_ref[k])
                both = dot(jnp.concatenate([r_hi, r_lo], 0), grad_ref[k])
                h_hi, h_lo = split2(both[:rank] + both[rank:])
                both = dot(jnp.concatenate([h_hi, h_lo], 0), tok_out[...])
                left_out[k] = left_ref[k] + both[:rank] + both[rank:]

    whole3 = lambda i, ids: (0, 0, 0)
    grid_spec = pltpu.PrefetchScalarGridSpec(
        num_scalar_prefetch=1,
        grid=(steps,),
        in_specs=[pl.BlockSpec((per, feats), lambda i, ids: (0, 0)) for _ in shards]
        + [pl.BlockSpec((block, per), lambda i, ids, j=j: (i, ids[j])) for j in range(count)]
        + [
            pl.BlockSpec((2, block, feats), lambda i, ids: (0, i, 0)),
            pl.BlockSpec((2, rank, rows), whole3),
            pl.BlockSpec((2, rank, feats), whole3),
        ],
        out_specs=[
            pl.BlockSpec((2, rows, width), whole3),
            pl.BlockSpec((width, feats), lambda i, ids: (0, 0)),
            pl.BlockSpec((2, rank, feats), whole3),
        ],
    )
    return pl.pallas_call(
        body,
        grid_spec=grid_spec,
        out_shape=[
            jax.ShapeDtypeStruct((2, rows, width), bf16),
            jax.ShapeDtypeStruct((width, feats), bf16),
            jax.ShapeDtypeStruct((2, rank, feats), f32),
        ],
        compiler_params=params(48, 1),
        cost_estimate=cost(2 * rows * feats * width, 2 * weight.size),
        name="forward_chunk",
    )(ids, *shards, *([upstream] * count), weight, right_t, left_in)


def gradient(grads, toks, feedback, block):
    _, rows, feats = feedback.shape
    count = len(grads)
    width = toks[0].shape[0]

    def body(*refs):
        grad_refs = refs[:count]
        tok_refs = refs[count : 2 * count]
        fb_ref, hi_ref, lo_ref = refs[2 * count :]
        acc = fb_ref[0]
        for g, t in zip(grad_refs, tok_refs):
            acc = acc + dot(g[0], t[...])
        hi, lo = split2(acc)
        hi_ref[0] = hi
        lo_ref[0] = lo

    out_spec = pl.BlockSpec((1, block, feats), lambda k, i: (k, i, 0))
    return pl.pallas_call(
        body,
        grid=(2, rows // block),
        in_specs=[pl.BlockSpec((1, block, width), lambda k, i: (k, i, 0)) for _ in grads]
        + [
            pl.BlockSpec((width, feats), lambda k, i: (0, 0), pipeline_mode=pl.Buffered(1))
            for _ in toks
        ]
        + [out_spec],
        out_specs=[out_spec, out_spec],
        out_shape=[jax.ShapeDtypeStruct(feedback.shape, bf16)] * 2,
        compiler_params=params(48, 2),
        cost_estimate=cost(2 * rows * feats * width * count, 8 * feedback.size),
        name="gradient",
    )(*grads, *toks, feedback)


def project(delta_hi, delta_lo, left_t, block=512):
    _, rows, feats = delta_hi.shape
    rank = left_t.shape[1]

    def body(hi_ref, lo_ref, l_ref, out_ref):
        d = pl.program_id(1)
        l_hi, l_lo = split2(l_ref[0])
        both = dot_nt(jnp.concatenate([l_hi, l_lo], 0), hi_ref[0])
        part = both[:rank] + both[rank:] + dot_nt(l_hi, lo_ref[0])

        @pl.when(d == 0)
        def _():
            out_ref[0] = part

        @pl.when(d > 0)
        def _():
            out_ref[0] += part

    return pl.pallas_call(
        body,
        grid=(2, feats // block),
        in_specs=[
            pl.BlockSpec((1, rows, block), lambda k, d: (k, 0, d)),
            pl.BlockSpec((1, rows, block), lambda k, d: (k, 0, d)),
            pl.BlockSpec((1, rank, block), lambda k, d: (k, 0, d)),
        ],
        out_specs=pl.BlockSpec((1, rank, rows), lambda k, d: (k, 0, 0)),
        out_shape=jax.ShapeDtypeStruct((2, rank, rows), f32),
        compiler_params=params(32, 2),
        cost_estimate=cost(2 * rows * feats * 256, 4 * delta_hi.size),
        name="project",
    )(delta_hi, delta_lo, left_t)


def factorize(left_t):
    _, rank, feats = left_t.shape

    def body(l_ref, inv_ref, cat_ref):
        row_id = lax.broadcasted_iota(jnp.int32, (rank, 1), 0)
        eye = (
            lax.broadcasted_iota(jnp.int32, (rank, rank), 0)
            == lax.broadcasted_iota(jnp.int32, (rank, rank), 1)
        ).astype(f32)
        work, scale = [], []
        for k in range(2):
            x = l_ref[k]
            gram = lax.dot_general(x, x, contract_last, precision=highest, preferred_element_type=f32)
            work.append(jnp.concatenate([gram, eye], 1))
            scale.append(jnp.zeros((rank, 1), f32))
        for j in range(rank):
            for k in range(2):
                a = work[k]
                pivot = a[j : j + 1, j : j + 1]
                ratio = jnp.where(row_id > j, a[:, j : j + 1] / pivot, 0.0)
                scale[k] = jnp.where(row_id == j, lax.rsqrt(pivot), scale[k])
                work[k] = a - ratio * a[j : j + 1, :]
        for k in range(2):
            inv = work[k][:, rank:] * scale[k]
            inv_ref[k] = inv
            basis = jnp.dot(inv, l_ref[k], precision=highest, preferred_element_type=f32)
            b_hi, b_lo = split2(basis)
            cat_ref[k] = jnp.concatenate([b_hi, b_lo, b_hi], 0)

    return pl.pallas_call(
        body,
        out_shape=[
            jax.ShapeDtypeStruct((2, rank, rank), f32),
            jax.ShapeDtypeStruct((2, 3 * rank, feats), bf16),
        ],
        compiler_params=pltpu.CompilerParams(vmem_limit_bytes=32 * MIB),
        cost_estimate=cost(2000000000, 4 * left_t.size),
        name="factorize",
    )(left_t)


def finish(slab, y_t, inverse, basis_cat, delta_hi, delta_lo, momentum, weight, replicas, block):
    _, rows, feats = delta_hi.shape
    rank = y_t.shape[1]
    cols = momentum.shape[2]

    def body(
        slab_ref, y_ref, inv_ref, cat_ref, cols_ref, hi_ref, lo_ref, mom_ref, w_ref,
        fb_out, mom_out, w_out, rn_out, rn_cat,
    ):
        i = pl.program_id(1)

        @pl.when(i == 0)
        def _():
            mean = y_ref[0] * (1.0 / replicas)
            rn_t = jnp.dot(inv_ref[0], mean, precision=highest, preferred_element_type=f32)
            rn_out[0] = rn_t
            hi, lo = split2(rn_t.T)
            rn_cat[...] = jnp.concatenate([hi, hi, lo], 1)

        part = rn_cat[pl.ds(pl.multiple_of(i * block, block), block), :]
        approx = dot(part, cat_ref[0])
        fb_out[0] = (hi_ref[0].astype(f32) - approx) + lo_ref[0].astype(f32)
        mom = momentum_decay * mom_ref[0] + dot(part, cols_ref[0])
        mom_out[0] = mom
        w_out[0] = (w_ref[0].astype(f32) - step_rate * mom).astype(bf16)

    wide = pl.BlockSpec((1, block, feats), lambda k, i, s: (k, i, 0))
    thin = pl.BlockSpec((1, block, cols), lambda k, i, s: (k, i, 0))
    grid_spec = pltpu.PrefetchScalarGridSpec(
        num_scalar_prefetch=1,
        grid=(2, rows // block),
        in_specs=[
            pl.BlockSpec((1, rank, rows), lambda k, i, s: (k, 0, 0)),
            pl.BlockSpec((1, rank, rank), lambda k, i, s: (k, 0, 0)),
            pl.BlockSpec((1, 3 * rank, feats), lambda k, i, s: (k, 0, 0)),
            pl.BlockSpec((1, 3 * rank, cols), lambda k, i, s: (k, 0, s[0])),
            wide,
            wide,
            thin,
            pl.BlockSpec((1, block, cols), lambda k, i, s: (k, i, s[0])),
        ],
        out_specs=[
            wide,
            thin,
            thin,
            pl.BlockSpec((1, rank, rows), lambda k, i, s: (k, 0, 0)),
        ],
        scratch_shapes=[pltpu.VMEM((rows, 3 * rank), bf16)],
    )
    return pl.pallas_call(
        body,
        grid_spec=grid_spec,
        out_shape=[
            jax.ShapeDtypeStruct((2, rows, feats), f32),
            jax.ShapeDtypeStruct((2, rows, cols), f32),
            jax.ShapeDtypeStruct((2, rows, cols), bf16),
            jax.ShapeDtypeStruct((2, rank, rows), f32),
        ],
        compiler_params=params(48, 2),
        cost_estimate=cost(2 * rows * feats * 256, 8 * delta_hi.size),
        name="finish",
    )(slab, y_t, inverse, basis_cat, basis_cat, delta_hi, delta_lo, momentum, weight)


def swap(x, axis, mask):
    size = lax.axis_size(axis)
    return lax.ppermute(x, axis, [(i, i ^ mask) for i in range(size)])


def halve(x, me, mask):
    width = x.shape[1] // 2
    bit = ((me & mask) != 0).astype(jnp.int32)
    keep = lax.dynamic_slice_in_dim(x, bit * width, width, 1)
    send = lax.dynamic_slice_in_dim(x, (1 - bit) * width, width, 1)
    return keep + swap(send, "fsdp", mask)


def double(x, me, mask):
    other = swap(x, "fsdp", mask)
    low = (me & mask) == 0
    return jnp.concatenate([jnp.where(low, x, other), jnp.where(low, other, x)], 1)


def left_total(left_t, me):
    fsdp, rep = lax.axis_size("fsdp"), lax.axis_size("rep")
    masks = [1 << b for b in range(1, fsdp.bit_length() - 1)]
    rep_masks = [(2 << b) - 1 for b in range(rep.bit_length() - 1)]
    core = me & 1
    keep = lax.dynamic_index_in_dim(left_t, core, 0, keepdims=False)
    send = lax.dynamic_index_in_dim(left_t, 1 - core, 0, keepdims=False)
    mine = keep + swap(send, "fsdp", 1)
    half = mine.shape[0] // 2
    pieces = [mine[:half], mine[half:]]
    orders = [masks, masks[::-1]]
    for step in range(len(masks)):
        pieces = [halve(p, me, o[step]) for p, o in zip(pieces, orders)]
    pieces = rep_total(pieces)
    for step in reversed(range(len(masks))):
        pieces = [double(p, me, o[step]) for p, o in zip(pieces, orders)]
    mine = jnp.concatenate(pieces, 0)
    other = swap(mine, "fsdp", 1)
    return jnp.where(core == 0, jnp.stack([mine, other]), jnp.stack([other, mine]))


def rep_total(pieces):
    rep = lax.axis_size("rep")
    masks = [(2 << b) - 1 for b in range(rep.bit_length() - 1)]
    for step in range(len(masks)):
        pieces = [
            p + swap(p, "rep", o[step]) for p, o in zip(pieces, [masks, masks[::-1]])
        ]
    return pieces


def row_block(rows, most):
    return max(b for b in range(16, min(rows, most) + 1, 16) if rows % b == 0)


def per_device(tokens, upstream, weight, feedback, momentum, right_factor):
    fsdp, replicas = lax.axis_size("fsdp"), lax.axis_size("rep")
    me = lax.axis_index("fsdp")
    rows = weight.shape[1]
    own = tokens[0]
    per = own.shape[0]
    inner = [1 << b for b in range(fsdp.bit_length() - 3)]
    far_x, far_y = fsdp // 4, fsdp // 2
    right_t = jnp.swapaxes(right_factor, 1, 2)

    def gather_inner(shard):
        parts, offsets = [shard], [0]
        for m in inner:
            parts = parts + [swap(p, "fsdp", m) for p in parts]
            offsets = offsets + [o ^ m for o in offsets]
        return parts, offsets

    got_x = swap(own, "fsdp", far_x)
    got_y = swap(own, "fsdp", far_y)
    half = per // 2
    got_d = jnp.concatenate(
        [swap(got_x[:half], "fsdp", far_y), swap(got_y[half:], "fsdp", far_x)], 0
    )
    left_t = feedback_left(feedback[0], right_t)
    grads, toks = [], []
    for shard, base in ((own, 0), (got_x, far_x), (got_y, far_y), (got_d, far_x ^ far_y)):
        parts, offsets = gather_inner(shard)
        ids = jnp.stack([me ^ (base ^ o) for o in offsets]).astype(jnp.int32)
        grad, tok, left_t = forward_chunk(
            ids, parts, weight, upstream[0], right_t, left_t, row_block(rows, 448)
        )
        grads.append(grad)
        toks.append(tok)
    total_t = left_total(left_t, me) * (1.0 / replicas)
    delta_hi, delta_lo = gradient(grads, toks, feedback[0], row_block(rows, 224))
    y_t = project(delta_hi, delta_lo, total_t)
    y_t = jnp.stack(rep_total([y_t[0], y_t[1]]))
    inverse, basis_cat = factorize(total_t)
    slab = lax.axis_index("rep").astype(jnp.int32).reshape(1)
    feedback_next, momentum_next, weight_next, rn_t = finish(
        slab, y_t, inverse, basis_cat, delta_hi, delta_lo, momentum, weight, replicas,
        row_block(rows, 224),
    )
    return (feedback_next[None], momentum_next, weight_next, jnp.swapaxes(rn_t, 1, 2))


def solution(mesh):
    placed = (
        P("rep", "fsdp", None),
        P("rep", "fsdp", None),
        P(None, "fsdp", None),
        P("rep", None, "fsdp", None),
        P(None, "fsdp", "rep"),
        P(None, "fsdp", None),
    )
    return jax.shard_map(
        per_device,
        mesh=mesh,
        in_specs=placed,
        out_specs=(
            P("rep", None, "fsdp", None),
            P(None, "fsdp", "rep"),
            P(None, "fsdp", "rep"),
            P(None, "fsdp", None),
        ),
        check_vma=False,
    )
```

```python
import jax
import jax.numpy as jnp
from jax import lax
from jax.experimental import pallas as pl
from jax.experimental.pallas import tpu as pltpu
from jax.sharding import PartitionSpec as P

momentum_decay = 0.9
step_rate = 0.05
highest = lax.Precision.HIGHEST
f32 = jnp.float32
bf16 = jnp.bfloat16
contract_last = (((1,), (1,)), ((), ()))
MIB = 1024 * 1024
vmem = pl.BlockSpec(memory_space=pltpu.VMEM)
smem = pl.BlockSpec(memory_space=pltpu.SMEM)
anywhere = pl.BlockSpec(memory_space=pl.ANY)
hbm = pl.BlockSpec(memory_space=pltpu.HBM)


def split2(x):
    hi = x.astype(bf16)
    return hi, (x - hi.astype(f32)).astype(bf16)


def stacked(x):
    return jnp.concatenate(split2(x), 0)


def fold(x):
    half = x.shape[0] // 2
    return x[:half] + x[half:]


def dot(a, b):
    return jnp.dot(a, b, preferred_element_type=f32)


def dot_nt(a, b):
    return lax.dot_general(a, b, contract_last, preferred_element_type=f32)


def shape(*dims, dtype=f32):
    return jax.ShapeDtypeStruct(dims, dtype)


def call(body, place, operands, out_shape, mib, macs=0, **more):
    nbytes = sum(x.size * x.dtype.itemsize for x in operands)
    spec = dict(
        in_specs=[smem] + [vmem] * len(operands),
        out_specs=jax.tree.map(lambda _: vmem, out_shape),
    ) | more
    return pl.pallas_call(
        body,
        out_shape=out_shape,
        compiler_params=pltpu.CompilerParams(vmem_limit_bytes=mib * MIB),
        cost_estimate=pl.CostEstimate(flops=2 * macs, bytes_accessed=nbytes, transcendentals=0),
        **spec,
    )(place, *operands)


def divisor(size, most, unit):
    return max(b for b in range(unit, min(size, most) + 1, unit) if size % b == 0)


def span(i, size):
    return pl.ds(pl.multiple_of(i * size, size), size)


def grant(total, feats):
    return 16 if total * feats <= 4 * MIB else 28


def feedback_left(place, feedback, weight, right_t):
    _, rows, feats = feedback.shape
    rank = right_t.shape[1]
    block = 512
    steps = feats // block

    def body(place_ref, fb_ref, w_ref, r_ref, held_ref, held_w_ref, out_ref, sems, w_sems):
        def copy(k, d):
            cols = slice(d * block, (d + 1) * block)
            return pltpu.make_async_copy(
                fb_ref.at[k, :, cols], held_ref.at[k, :, cols], sems.at[k, d]
            )

        order = [(k, d) for k in range(2) for d in range(steps)]
        for k, d in order:
            copy(k, d).start()
        w_copies = [
            pltpu.make_async_copy(w_ref.at[k], held_w_ref.at[k], w_sems.at[k]) for k in range(2)
        ]
        for c in w_copies:
            c.start()
        for k, d in order:
            cols = slice(d * block, (d + 1) * block)
            r_cat = stacked(r_ref[k])
            copy(k, d).wait()
            fb_hi, fb_lo = split2(held_ref[k, :, cols])
            out_ref[k, :, cols] = fold(dot(r_cat, fb_hi)) + dot(r_cat[:rank], fb_lo)
        for c in w_copies:
            c.wait()

    return call(
        body, place, (feedback, weight, right_t),
        [shape(*feedback.shape), shape(*weight.shape, dtype=bf16), shape(2, rank, feats)], 16,
        2 * rows * feats * 256, name="feedback_left", in_specs=[smem, hbm, hbm, vmem],
        scratch_shapes=[pltpu.SemaphoreType.DMA((2, steps)), pltpu.SemaphoreType.DMA((2,))],
    )


def forward_chunk(place, parts, offsets, weight, upstream, right_t, left_in):
    count = len(parts)
    feats = parts[0].shape[1]
    width = sum(p.shape[0] for p in parts)
    per = width // len(offsets)
    rows = weight.shape[1]
    rank = right_t.shape[1]

    def body(place_ref, *refs):
        tok_refs, refs = refs[:count], refs[count:]
        w_ref, up_ref, r_ref, left_ref, grad_ref, tok_ref, left_out = refs
        me = place_ref[0]
        at = 0
        for t in tok_refs:
            tok_ref[at : at + t.shape[0], :] = t[...]
            at += t.shape[0]
        gate_pre = dot_nt(w_ref[0], tok_ref[...])
        up_pre = dot_nt(w_ref[1], tok_ref[...])
        cot = jnp.concatenate([up_ref[:, span(me ^ o, per)] for o in offsets], 1).astype(f32)
        s = jax.nn.sigmoid(gate_pre)
        cot_s = cot * s
        grad_ref[0] = (cot_s * up_pre * (1.0 + gate_pre * (1.0 - s))).astype(bf16)
        grad_ref[1] = (cot_s * gate_pre).astype(bf16)
        for k in range(2):
            h = fold(dot(stacked(r_ref[k]), grad_ref[k]))
            left_out[k] = left_ref[k] + fold(dot(stacked(h), tok_ref[...]))

    return call(
        body, place, (*parts, weight, upstream, right_t, left_in),
        [shape(2, rows, width, dtype=bf16), shape(width, feats, dtype=bf16), shape(2, rank, feats)],
        grant(width, feats), 2 * rows * feats * width, name="forward_chunk",
    )


def gradient(place, delta, grads, toks, k, part, parts):
    _, rows, feats = delta.shape
    total = sum(t.shape[0] for t in toks)
    block = feats // parts
    cols = slice(part * block, (part + 1) * block)
    count = len(toks)

    def body(place_ref, fb_ref, *refs):
        acc = fb_ref[k, :, cols]
        for g, t in zip(refs[:count], refs[count : 2 * count]):
            acc = acc + dot(g[k], t[:, cols])
        refs[2 * count][k, :, cols] = acc

    return call(
        body, place, (delta, *grads, *toks), shape(*delta.shape), grant(total // 2, feats),
        rows * block * total, name="gradient", input_output_aliases={1: 0},
    )


def project(place, delta, mine, other, k, scale):
    _, rows, feats = delta.shape
    rank = mine.shape[0]
    block = 512

    def body(place_ref, delta_ref, mine_ref, other_ref, out_ref):
        own = (place_ref[0] & 1) == k
        acc = None
        for d in range(feats // block):
            cols = slice(d * block, (d + 1) * block)
            cat = stacked(jnp.where(own, mine_ref[:, cols], other_ref[:, cols]) * scale)
            hi, lo = split2(delta_ref[k, :, cols])
            part = fold(dot_nt(cat, hi)) + dot_nt(cat[:rank], lo)
            acc = part if acc is None else acc + part
        out_ref[...] = acc

    return call(
        body, place, (delta, mine, other), shape(rank, rows), 16, rows * feats * 256, name="project"
    )


def factorize(place, mine, other, scale):
    rank, feats = mine.shape

    def body(place_ref, mine_ref, other_ref, inv_ref):
        core = place_ref[0] & 1
        row_id = lax.broadcasted_iota(jnp.int32, (rank, 1), 0)
        eye = (
            lax.broadcasted_iota(jnp.int32, (rank, rank), 0)
            == lax.broadcasted_iota(jnp.int32, (rank, rank), 1)
        ).astype(f32)
        work, roots = [], []
        for k in range(2):
            x = jnp.where(core == k, mine_ref[...], other_ref[...]) * scale
            gram = lax.dot_general(x, x, contract_last, precision=highest, preferred_element_type=f32)
            work.append(jnp.concatenate([gram, eye], 1))
            roots.append(jnp.zeros((rank, 1), f32))
        for j in range(rank):
            for k in range(2):
                a = work[k]
                pivot = a[j : j + 1, j : j + 1]
                ratio = jnp.where(row_id > j, a[:, j : j + 1] / pivot, 0.0)
                roots[k] = jnp.where(row_id == j, lax.rsqrt(pivot), roots[k])
                work[k] = a - ratio * a[j : j + 1, :]
        for k in range(2):
            inv_ref[k] = work[k][:, rank:] * roots[k]

    return call(
        body, place, (mine, other), shape(2, rank, rank), 8, 1000000000, name="factorize"
    )


def make_basis(place, mine, other, inverse, scale):
    rank, feats = mine.shape

    def body(place_ref, mine_ref, other_ref, inv_ref, cat_ref):
        core = place_ref[0] & 1
        for k in range(2):
            x = jnp.where(core == k, mine_ref[...], other_ref[...]) * scale
            basis = jnp.dot(inv_ref[k], x, precision=highest, preferred_element_type=f32)
            b_hi, b_lo = split2(basis)
            cat_ref[k] = jnp.concatenate([b_hi, b_lo, b_hi], 0)

    return call(
        body, place, (mine, other, inverse), shape(2, 3 * rank, feats, dtype=bf16), 8, 500000000,
        name="make_basis",
    )


def finish(place, ys, gots, inverse, basis_cat, delta, momentum, weight, replicas):
    _, rows, feats = delta.shape
    rank = ys[0].shape[0]
    cols = momentum.shape[2]
    block = divisor(rows, 128, 16)
    steps = rows // block
    slots = min(4, 2 * steps)

    def body(
        place_ref, y0_ref, y1_ref, got0_ref, got1_ref, inv_ref, cat_ref, delta_ref, mom_ref, w_ref,
        fb_out, mom_out, w_out, rn_out, rn_cat, fb_slot, mom_slot, w_slot, sems,
    ):
        slab = span(place_ref[1], cols)
        for k, (y_ref, got_ref) in enumerate(((y0_ref, got0_ref), (y1_ref, got1_ref))):
            mean = (y_ref[...] + got_ref[...]) * (1.0 / replicas)
            rn_t = jnp.dot(inv_ref[k], mean, precision=highest, preferred_element_type=f32)
            rn_out[k] = rn_t
            hi, lo = split2(rn_t.T)
            rn_cat[k] = jnp.concatenate([hi, hi, lo], 1)

        def copies(i):
            k, at, slot = i // steps, span(i % steps, block), i % slots
            return [
                pltpu.make_async_copy(src.at[slot], dst.at[k, at, :], sems.at[j, slot])
                for j, (src, dst) in enumerate(
                    ((fb_slot, fb_out), (mom_slot, mom_out), (w_slot, w_out))
                )
            ]

        def step(i, _):
            k, at, slot = i // steps, span(i % steps, block), i % slots

            @pl.when(i >= slots)
            def _():
                for c in copies(i - slots):
                    c.wait()

            part = rn_cat[k, at, :]
            fb_slot[slot] = delta_ref[k, at, :] - dot(part, cat_ref[k])
            mom = momentum_decay * mom_ref[k, at, :] + dot(part, cat_ref[k, :, slab])
            mom_slot[slot] = mom
            w_slot[slot] = (w_ref[k, at, slab].astype(f32) - step_rate * mom).astype(bf16)
            for c in copies(i):
                c.start()
            return 0

        lax.fori_loop(0, 2 * steps, step, 0)
        for i in range(2 * steps - slots, 2 * steps):
            for c in copies(i):
                c.wait()

    return call(
        body, place, (*ys, *gots, inverse, basis_cat, delta, momentum, weight),
        [
            shape(2, rows, feats), shape(2, rows, cols),
            shape(2, rows, cols, dtype=bf16), shape(2, rank, rows),
        ],
        16, 2 * rows * feats * 256, name="finish",
        out_specs=[anywhere, anywhere, anywhere, vmem],
        scratch_shapes=[
            pltpu.VMEM((2, rows, 3 * rank), bf16),
            pltpu.VMEM((slots, block, feats), f32),
            pltpu.VMEM((slots, block, cols), f32),
            pltpu.VMEM((slots, block, cols), bf16),
            pltpu.SemaphoreType.DMA((3, slots)),
        ],
    )


def swap(x, axis, mask):
    size = lax.axis_size(axis)
    return lax.ppermute(x, axis, [(i, i ^ mask) for i in range(size)])


def after(x, *others):
    return lax.optimization_barrier((x, *others))[0]


def has(place_ref, mask):
    return (place_ref[0] & mask) != 0


def by_core(place, left_t):
    _, rank, feats = left_t.shape

    def body(place_ref, left_ref, keep_ref, send_ref):
        odd = has(place_ref, 1)
        keep_ref[...] = jnp.where(odd, left_ref[1], left_ref[0])
        send_ref[...] = jnp.where(odd, left_ref[0], left_ref[1])

    return call(body, place, (left_t,), [shape(rank, feats)] * 2, 4, name="by_core")


def add(place, mine, got, masks=None):
    count = len(mine)

    def body(place_ref, *refs):
        outs = refs[2 * count :]
        for j in range(count):
            total = refs[j][...] + refs[count + j][...]
            if masks is None:
                outs[j][...] = total
                continue
            half = total.shape[1] // 2
            high = has(place_ref, masks[j])
            outs[j][...] = jnp.where(high, total[:, half:], total[:, :half])
            outs[count + j][...] = jnp.where(high, total[:, :half], total[:, half:])

    out = [shape(*x.shape) for x in mine]
    if masks is not None:
        out = [shape(x.shape[0], x.shape[1] // 2) for x in mine] * 2
    res = call(body, place, (*mine, *got), out, 4, name="add")
    return res if masks is None else (res[:count], res[count:])


def add_bands(place, keep, got, masks):
    rank, feats = keep.shape
    band, half = rank // 2, feats // 2

    def body(place_ref, keep_ref, got_ref, *outs):
        for j in range(2):
            at = slice(j * band, (j + 1) * band)
            total = keep_ref[at, :] + got_ref[at, :]
            high = has(place_ref, masks[j])
            outs[j][...] = jnp.where(high, total[:, half:], total[:, :half])
            outs[2 + j][...] = jnp.where(high, total[:, :half], total[:, half:])

    res = call(body, place, (keep, got), [shape(band, half)] * 4, 4, name="add_bands")
    return res[:2], res[2:]


def join(place, mine, got, masks, last):
    band, width = mine[0].shape

    def body(place_ref, a0, a1, b0, b1, *outs):
        for j, (a, b) in enumerate(((a0, b0), (a1, b1))):
            high = has(place_ref, masks[j])
            x, y = a[...], b[...]
            both = jnp.concatenate([jnp.where(high, y, x), jnp.where(high, x, y)], 1)
            if last:
                outs[0][j * band : (j + 1) * band, :] = both
            else:
                outs[j][...] = both

    out = [shape(2 * band, 2 * width)] if last else [shape(band, 2 * width)] * 2
    return call(body, place, (*mine, *got), out, 4, name="join")


def left_total(place, left_t, work):
    fsdp, rep = lax.axis_size("fsdp"), lax.axis_size("rep")
    masks = [1 << b for b in range(1, fsdp.bit_length() - 1)]
    orders = list(zip(masks, masks[::-1]))
    rep_masks = [(2 << b) - 1 for b in range(rep.bit_length() - 1)]

    def beside(sends, axis, step_masks, count):
        got = [swap(x, axis, m) for x, m in zip(sends, step_masks)]
        return lax.optimization_barrier((*got, work(sends, count)))[:-1]

    keep, send = by_core(place, left_t)
    got = swap(send, "fsdp", 1)
    keeps, sends = add_bands(place, keep, got, orders[0])
    for step in range(len(masks)):
        got = beside(sends, "fsdp", orders[step], 2 - min(step, 1))
        if step + 1 < len(masks):
            keeps, sends = add(place, keeps, got, orders[step + 1])
        else:
            pieces = add(place, keeps, got)
    for pair in zip(rep_masks, rep_masks[::-1]):
        pieces = add(place, pieces, beside(pieces, "rep", pair, 1))
    for step in reversed(range(len(masks))):
        got = beside(pieces, "fsdp", orders[step], 2 - min(step, 1))
        pieces = join(place, pieces, got, orders[step], step == 0)
    return pieces[0], swap(pieces[0], "fsdp", 1)


def per_device(tokens, upstream, weight, feedback, momentum, right_factor):
    fsdp, replicas = lax.axis_size("fsdp"), lax.axis_size("rep")
    place = jnp.stack([lax.axis_index("fsdp"), lax.axis_index("rep")]).astype(jnp.int32)
    own = tokens[0]
    per, feats = own.shape
    inner = [1 << b for b in range(fsdp.bit_length() - 3)]
    far_x, far_y = fsdp // 4, fsdp // 2
    right_t = jnp.swapaxes(right_factor, 1, 2)
    scale = 1.0 / replicas

    def gather_inner(parts, base):
        parts, offsets = list(parts), [base]
        for m in inner:
            parts = parts + [swap(p, "fsdp", m) for p in parts]
            offsets = offsets + [o ^ m for o in offsets]
        return parts, offsets

    def halves(x, y):
        def body(place_ref, x_ref, y_ref, x_out, y_out):
            x_out[...] = x_ref[: per // 2, :]
            y_out[...] = y_ref[per // 2 :, :]

        return call(body, place, (x, y), [shape(per // 2, feats, dtype=bf16)] * 2, 4, name="halves")

    grads, toks = [], []

    def forward(parts, offsets, left):
        grad, tok, left = forward_chunk(
            place, parts, offsets, held_weight, upstream[0], right_t, left
        )
        grads.append(grad)
        toks.append(tok)
        return left

    got_x = swap(own, "fsdp", far_x)
    got_y = swap(own, "fsdp", far_y)
    parts, offsets = gather_inner([own], 0)
    delta, held_weight, left_t = feedback_left(place, feedback[0], weight, right_t)
    left_t = forward(parts, offsets, left_t)
    got_x, got_y, left_t = lax.optimization_barrier((got_x, got_y, left_t))
    send_x, send_y = halves(got_x, got_y)
    far = [swap(send_x, "fsdp", far_y), swap(send_y, "fsdp", far_x)]
    parts_x, offsets_x = gather_inner([got_x], far_x)
    parts_y, offsets_y = gather_inner([got_y], far_y)
    left_t = forward(parts_x + parts_y, offsets_x + offsets_y, left_t)
    far_0, far_1, left_t = lax.optimization_barrier((*far, left_t))
    parts, offsets = gather_inner([far_0, far_1], far_x ^ far_y)
    left_t = forward(parts, offsets, left_t)

    pending = [(k, part) for k in range(2) for part in range(4)]

    def pieces(count):
        nonlocal delta
        for _ in range(min(count, len(pending))):
            k, part = pending.pop(0)
            delta = gradient(place, delta, grads, toks, k, part, 4)

    def work(sends, count):
        nonlocal delta
        delta = after(delta, *sends)
        pieces(count)
        return delta

    mine, other = left_total(place, left_t, work)
    pieces(len(pending))
    y = [project(place, delta, mine, other, k, scale) for k in range(2)]
    masks = [(2 << b) - 1 for b in range(replicas.bit_length() - 1)]
    for step, pair in enumerate(zip(masks, masks[::-1])):
        got = [swap(p, "rep", m) for p, m in zip(y, pair)]
        if step == 0:
            inverse = factorize(place, after(mine, *y), other, scale)
            got = lax.optimization_barrier((*got, inverse))[:-1]
        if step == 1:
            basis_cat = make_basis(place, after(mine, *y), other, inverse, scale)
        if step + 1 < len(masks):
            y = add(place, y, got)
    feedback_next, momentum_next, weight_next, rn_t = finish(
        place, y, got, inverse, basis_cat, delta, momentum, held_weight, replicas
    )
    return (feedback_next[None], momentum_next, weight_next, jnp.swapaxes(rn_t, 1, 2))


def solution(mesh):
    placed = (
        P("rep", "fsdp", None),
        P("rep", "fsdp", None),
        P(None, "fsdp", None),
        P("rep", None, "fsdp", None),
        P(None, "fsdp", "rep"),
        P(None, "fsdp", None),
    )
    return jax.shard_map(
        per_device,
        mesh=mesh,
        in_specs=placed,
        out_specs=(
            P("rep", None, "fsdp", None),
            P(None, "fsdp", "rep"),
            P(None, "fsdp", "rep"),
            P(None, "fsdp", None),
        ),
        check_vma=False,
    )
```

```python
import jax
import jax.numpy as jnp
from jax import lax
from jax.experimental import pallas as pl
from jax.experimental.pallas import tpu as pltpu
from jax.sharding import PartitionSpec as P

momentum_decay = 0.9
step_rate = 0.05
highest = lax.Precision.HIGHEST
f32 = jnp.float32
bf16 = jnp.bfloat16
contract_last = (((1,), (1,)), ((), ()))
MIB = 1024 * 1024
vmem = pl.BlockSpec(memory_space=pltpu.VMEM)
smem = pl.BlockSpec(memory_space=pltpu.SMEM)
anywhere = pl.BlockSpec(memory_space=pl.ANY)
hbm = pl.BlockSpec(memory_space=pltpu.HBM)


def kept(like):
    return pltpu.VMEM(like.shape, like.dtype)


def in_vmem(x):
    return pltpu.with_memory_space_constraint(x, pltpu.VMEM)


def in_hbm(x):
    return pltpu.with_memory_space_constraint(x, pltpu.HBM)


def split2(x):
    hi = x.astype(bf16)
    return hi, (x - hi.astype(f32)).astype(bf16)


def stacked(x):
    return jnp.concatenate(split2(x), 0)


def fold(x):
    half = x.shape[0] // 2
    return x[:half] + x[half:]


def dot(a, b):
    return jnp.dot(a, b, preferred_element_type=f32)


def dot_nt(a, b):
    return lax.dot_general(a, b, contract_last, preferred_element_type=f32)


def shape(*dims, dtype=f32):
    return jax.ShapeDtypeStruct(dims, dtype)


def call(body, place, operands, out_shape, mib, macs=0, **more):
    nbytes = sum(x.size * x.dtype.itemsize for x in operands)
    spec = dict(
        in_specs=[smem] + [vmem] * len(operands),
        out_specs=jax.tree.map(lambda _: vmem, out_shape),
    ) | more
    return pl.pallas_call(
        body,
        out_shape=out_shape,
        compiler_params=pltpu.CompilerParams(vmem_limit_bytes=mib * MIB),
        cost_estimate=pl.CostEstimate(flops=2 * macs, bytes_accessed=nbytes, transcendentals=0),
        **spec,
    )(place, *operands)


def divisor(size, most, unit):
    return max(b for b in range(unit, min(size, most) + 1, unit) if size % b == 0)


def span(i, size):
    return pl.ds(pl.multiple_of(i * size, size), size)


def grant(total, feats):
    return 14 if total * feats <= 4 * MIB else 28


def feedback_left(place, feedback, right_t):
    _, rows, feats = feedback.shape
    rank = right_t.shape[1]
    block = 512
    steps = feats // block

    def body(place_ref, fb_ref, r_ref, held_ref, out_ref, sems):
        def copy(k, d):
            cols = slice(d * block, (d + 1) * block)
            return pltpu.make_async_copy(
                fb_ref.at[k, :, cols], held_ref.at[k, :, cols], sems.at[k, d]
            )

        order = [(k, d) for k in range(2) for d in range(steps)]
        for k, d in order:
            copy(k, d).start()
        for k, d in order:
            cols = slice(d * block, (d + 1) * block)
            r_cat = stacked(r_ref[k])
            copy(k, d).wait()
            fb_hi, fb_lo = split2(held_ref[k, :, cols])
            out_ref[k, :, cols] = fold(dot(r_cat, fb_hi)) + dot(r_cat[:rank], fb_lo)

    return call(
        body, place, (in_hbm(feedback), right_t), [kept(feedback), shape(2, rank, feats)], 10,
        2 * rows * feats * 256, name="feedback_left", in_specs=[smem, hbm, vmem],
        scratch_shapes=[pltpu.SemaphoreType.DMA((2, steps))],
    )


def left_part(right, grad, tok):
    return fold(dot(stacked(fold(dot(stacked(right), grad))), tok))


def forward_chunk(place, parts, offsets, weight, upstream, right_t, left_in, last=False):
    count = len(parts)
    feats = parts[0].shape[1]
    width = sum(p.shape[0] for p in parts)
    per = width // len(offsets)
    rows = weight.shape[1]
    rank = right_t.shape[1]

    def body(place_ref, *refs):
        tok_refs, refs = refs[:count], refs[count:]
        w_ref, up_ref, r_ref, left_ref, grad_ref, tok_ref, left_out = refs
        me = place_ref[0]
        at = 0
        for t in tok_refs:
            tok_ref[at : at + t.shape[0], :] = t[...]
            at += t.shape[0]
        gate_pre = dot_nt(w_ref[0], tok_ref[...])
        up_pre = dot_nt(w_ref[1], tok_ref[...])
        cot = jnp.concatenate([up_ref[:, span(me ^ o, per)] for o in offsets], 1).astype(f32)
        s = jax.nn.sigmoid(gate_pre)
        cot_s = cot * s
        grad_ref[0] = (cot_s * up_pre * (1.0 + gate_pre * (1.0 - s))).astype(bf16)
        grad_ref[1] = (cot_s * gate_pre).astype(bf16)
        if last:
            k = (me & 1) ^ 1
            left_out[...] = left_ref[k] + left_part(r_ref[k], grad_ref[k], tok_ref[...])
        else:
            for k in range(2):
                left_out[k] = left_ref[k] + left_part(r_ref[k], grad_ref[k], tok_ref[...])

    return call(
        body, place, (*parts, weight, upstream, right_t, left_in),
        [
            shape(2, rows, width, dtype=bf16), shape(width, feats, dtype=bf16),
            shape(rank, feats) if last else shape(2, rank, feats),
        ],
        grant(width, feats), 2 * rows * feats * width, name="forward_chunk",
    )


def keep_left(place, right_t, grad, tok, left_in):
    _, rank, feats = left_in.shape

    def body(place_ref, r_ref, g_ref, t_ref, left_ref, out_ref):
        k = place_ref[0] & 1
        out_ref[...] = left_ref[k] + left_part(r_ref[k], g_ref[k], t_ref[...])

    return call(
        body, place, (right_t, grad, tok, left_in), shape(rank, feats), 8,
        grad.size * rank, name="keep_left",
    )


def gradient(place, delta, grads, toks, start, stop):
    _, rows, feats = delta.shape
    total = sum(t.shape[0] for t in toks)
    block = 256
    count = len(toks)

    def body(place_ref, fb_ref, *refs):
        for at in range(start, stop, block):
            cols = slice(at, at + block)
            for k in range(2):
                acc = fb_ref[k, :, cols]
                for g, t in zip(refs[:count], refs[count : 2 * count]):
                    acc = acc + dot(g[k], t[:, cols])
                refs[2 * count][k, :, cols] = acc

    return call(
        body, place, (in_vmem(delta), *grads, *toks), kept(delta),
        min(8, grant(total // 2, feats)), 2 * rows * (stop - start) * total,
        name="gradient", input_output_aliases={1: 0},
    )


def project(place, delta, left_t, flip, scale):
    _, rows, feats = delta.shape
    rank = left_t.shape[0]
    block = 512

    def body(place_ref, delta_ref, left_ref, *outs):
        k = (place_ref[0] & 1) ^ flip
        acc = None
        for d in range(feats // block):
            cols = slice(d * block, (d + 1) * block)
            cat = stacked(left_ref[:, cols] * scale)
            hi, lo = split2(delta_ref[k, :, cols])
            part = fold(dot_nt(cat, hi)) + dot_nt(cat[:rank], lo)
            acc = part if acc is None else acc + part
        outs[0][...] = acc[: rank // 2]
        outs[1][...] = acc[rank // 2 :]

    return call(
        body, place, (in_vmem(delta), left_t), [shape(rank // 2, rows)] * 2, 8, rows * feats * 256,
        name="project",
    )


def factorize(place, mine, other, scale):
    rank, feats = mine.shape

    def body(place_ref, mine_ref, other_ref, inv_ref):
        core = place_ref[0] & 1
        row_id = lax.broadcasted_iota(jnp.int32, (rank, 2 * rank), 0)
        eye = (
            lax.broadcasted_iota(jnp.int32, (rank, rank), 0)
            == lax.broadcasted_iota(jnp.int32, (rank, rank), 1)
        ).astype(f32)
        work, roots = [], []
        for k in range(2):
            x = jnp.where(core == k, mine_ref[...], other_ref[...]) * scale
            gram = lax.dot_general(x, x, contract_last, precision=highest, preferred_element_type=f32)
            work.append(jnp.concatenate([gram, eye], 1))
            roots.append(jnp.zeros((rank, 2 * rank), f32))
        group = 4
        for first in range(0, rank, group):
            for k in range(2):
                a = work[k]
                columns = [
                    jnp.broadcast_to(a[:, j : j + 1], a.shape) for j in range(first, first + group)
                ]
                for t in range(group):
                    j = first + t
                    pivot = columns[t][j : j + 1, :]
                    ratio = jnp.where(row_id > j, columns[t] * (1.0 / pivot), 0.0)
                    for u in range(t + 1, group):
                        columns[u] = columns[u] - ratio * columns[u][j : j + 1, :]
                    roots[k] = jnp.where(row_id == j, lax.rsqrt(pivot), roots[k])
                    a = a - ratio * a[j : j + 1, :]
                work[k] = a
        for k in range(2):
            inv_ref[k] = (work[k] * roots[k])[:, rank:]

    return call(
        body, place, (mine, other), shape(2, rank, rank), 8, 1000000000, name="factorize"
    )


def make_basis(place, mine, other, inverse, scale):
    rank, feats = mine.shape

    def body(place_ref, mine_ref, other_ref, inv_ref, cat_ref):
        core = place_ref[0] & 1
        for k in range(2):
            x = jnp.where(core == k, mine_ref[...], other_ref[...]) * scale
            basis = jnp.dot(inv_ref[k], x, precision=highest, preferred_element_type=f32)
            b_hi, b_lo = split2(basis)
            cat_ref[k] = jnp.concatenate([b_hi, b_lo, b_hi], 0)

    return call(
        body, place, (mine, other, inverse), shape(2, 3 * rank, feats, dtype=bf16), 8, 500000000,
        name="make_basis",
    )


def finish(place, ys, gots, inverse, basis_cat, delta, momentum, weight, replicas, flip, outs):
    _, rows, feats = delta.shape
    rank = inverse.shape[1]
    cols = momentum.shape[2]
    block = divisor(rows, 128, 16)
    steps = rows // block
    slots = min(4, steps)
    held = () if outs is None else tuple(outs)

    def body(
        place_ref, y0_ref, y1_ref, got0_ref, got1_ref, inv_ref, cat_ref, delta_ref, mom_ref, w_ref, *refs
    ):
        fb_out, mom_out, w_out, rn_out = refs[len(held) : len(held) + 4]
        rn_t, rn_cat, fb_slot, mom_slot, w_slot, sems, rn_sem = refs[len(held) + 4 :]
        slab = span(place_ref[1], cols)
        k = (place_ref[0] & 1) ^ flip
        mean = jnp.concatenate([y0_ref[...] + got0_ref[...], y1_ref[...] + got1_ref[...]], 0)
        rn_t[...] = jnp.dot(
            inv_ref[k], mean * (1.0 / replicas), precision=highest, preferred_element_type=f32
        )
        rn_copy = pltpu.make_async_copy(rn_t, rn_out.at[k], rn_sem)
        rn_copy.start()
        hi, lo = split2(rn_t[...].T)
        rn_cat[...] = jnp.concatenate([hi, hi, lo], 1)

        def copies(i):
            at, slot = slice(i * block, (i + 1) * block), i % slots
            return [
                pltpu.make_async_copy(src.at[slot], dst.at[k, at, :], sems.at[j, slot])
                for j, (src, dst) in enumerate(
                    ((fb_slot, fb_out), (mom_slot, mom_out), (w_slot, w_out))
                )
            ]

        for i in range(steps):
            at, slot = slice(i * block, (i + 1) * block), i % slots
            if i >= slots:
                for c in copies(i - slots):
                    c.wait()
            part = rn_cat[at, :]
            fb_slot[slot] = delta_ref[k, at, :] - dot(part, cat_ref[k])
            mom = momentum_decay * mom_ref[k, at, :] + dot(part, cat_ref[k, :, slab])
            mom_slot[slot] = mom
            w_slot[slot] = (w_ref[k, at, slab].astype(f32) - step_rate * mom).astype(bf16)
            for c in copies(i):
                c.start()
        for i in range(steps - slots, steps):
            for c in copies(i):
                c.wait()
        rn_copy.wait()

    operands = (*ys, *gots, inverse, basis_cat, in_vmem(delta), momentum, weight)
    return call(
        body, place, (*operands, *held),
        [
            shape(2, rows, feats), shape(2, rows, cols),
            shape(2, rows, cols, dtype=bf16), shape(2, rank, rows),
        ],
        10, rows * feats * 256, name="finish",
        in_specs=[smem] + [vmem] * len(operands) + [hbm] * len(held),
        out_specs=[hbm] * 4,
        input_output_aliases={1 + len(operands) + i: i for i in range(len(held))},
        scratch_shapes=[
            pltpu.VMEM((rank, rows), f32),
            pltpu.VMEM((rows, 3 * rank), bf16),
            pltpu.VMEM((slots, block, feats), f32),
            pltpu.VMEM((slots, block, cols), f32),
            pltpu.VMEM((slots, block, cols), bf16),
            pltpu.SemaphoreType.DMA((3, slots)),
            pltpu.SemaphoreType.DMA,
        ],
    )


def swap(x, axis, mask):
    size = lax.axis_size(axis)
    return lax.ppermute(x, axis, [(i, i ^ mask) for i in range(size)])


def after(x, *others):
    return lax.optimization_barrier((x, *others))[0]


def has(place_ref, mask):
    return (place_ref[0] & mask) != 0


def tree(terms):
    while len(terms) > 1:
        terms = [a + b for a, b in zip(terms[::2], terms[1::2])]
    return terms[0]


def add(place, terms):
    def body(place_ref, *refs):
        refs[-1][...] = tree([r[...] for r in refs[:-1]])

    return call(body, place, terms, shape(*terms[0].shape), 4, name="add")


def add_pairs(place, ours, gots):
    count = len(ours)

    def body(place_ref, *refs):
        for j in range(count):
            refs[2 * count + j][...] = refs[j][...] + refs[count + j][...]

    out = [shape(*x.shape) for x in ours]
    return call(body, place, (*ours, *gots), out, 4, name="add_pairs")


def part_of(place_ref, mask=0):
    return (place_ref[0] ^ mask) // 2


def add_cores(place, keep, got, parts):
    rank, feats = keep.shape
    width = feats // parts

    def body(place_ref, keep_ref, got_ref, *outs):
        for m, out in enumerate(outs):
            cols = span(part_of(place_ref, 2 * m), width)
            out[...] = keep_ref[:, cols] + got_ref[:, cols]

    return call(body, place, (keep, got), [shape(rank, width)] * parts, 4, name="add_cores")


def join(place, pieces):
    rank, width = pieces[0].shape

    def body(place_ref, *refs):
        for m, piece in enumerate(refs[:-1]):
            refs[-1][:, span(part_of(place_ref, 2 * m), width)] = piece[...]

    return call(body, place, pieces, shape(rank, width * len(pieces)), 4, name="join")


def left_total(place, keep, got, work):
    fsdp, rep = lax.axis_size("fsdp"), lax.axis_size("rep")
    parts = fsdp // 2

    def beside(sends, axis, masks, i):
        got = [swap(x, axis, m) for x, m in zip(sends, masks)]
        return list(lax.optimization_barrier((*got, work(sends, i)))[:-1])

    far = range(2, fsdp, 2)
    mine, *sends = add_cores(place, keep, got, parts)
    mine = add(place, [mine] + beside(sends, "fsdp", far, 0))
    mine = add(place, [mine] + beside([mine] * (rep - 1), "rep", range(1, rep), 1))
    mine = join(place, [mine] + beside([mine] * (parts - 1), "fsdp", far, 2))
    return mine, swap(mine, "fsdp", 1)


def per_device(tokens, upstream, weight, feedback, momentum, right_factor):
    fsdp, replicas = lax.axis_size("fsdp"), lax.axis_size("rep")
    place = jnp.stack([lax.axis_index("fsdp"), lax.axis_index("rep")]).astype(jnp.int32)
    own = tokens[0]
    per, feats = own.shape
    inner = [1 << b for b in range(fsdp.bit_length() - 3)]
    far_x, far_y = fsdp // 4, fsdp // 2
    right_t = jnp.swapaxes(right_factor, 1, 2)
    scale = 1.0 / replicas

    def gather_inner(parts, base):
        parts, offsets = list(parts), [base]
        for m in inner:
            parts = parts + [swap(p, "fsdp", m) for p in parts]
            offsets = offsets + [o ^ m for o in offsets]
        return parts, offsets

    def halves(x, y):
        def body(place_ref, x_ref, y_ref, x_out, y_out):
            x_out[...] = x_ref[: per // 2, :]
            y_out[...] = y_ref[per // 2 :, :]

        return call(body, place, (x, y), [shape(per // 2, feats, dtype=bf16)] * 2, 4, name="halves")

    grads, toks = [], []

    def forward(parts, offsets, left, last=False):
        grad, tok, left = forward_chunk(
            place, parts, offsets, weight, upstream[0], right_t, left, last
        )
        grads.append(grad)
        toks.append(tok)
        return left

    got_x = swap(own, "fsdp", far_x)
    got_y = swap(own, "fsdp", far_y)
    parts, offsets = gather_inner([own], 0)
    delta, left_t = feedback_left(place, feedback[0], right_t)
    left_t = forward(parts, offsets, left_t)
    got_x, got_y, left_t = lax.optimization_barrier((got_x, got_y, left_t))
    send_x, send_y = halves(got_x, got_y)
    far = [swap(send_x, "fsdp", far_y), swap(send_y, "fsdp", far_x)]
    parts_x, offsets_x = gather_inner([got_x], far_x)
    parts_y, offsets_y = gather_inner([got_y], far_y)
    left_t = forward(parts_x + parts_y, offsets_x + offsets_y, left_t)
    far_0, far_1, left_t = lax.optimization_barrier((*far, left_t))
    parts, offsets = gather_inner([far_0, far_1], far_x ^ far_y)
    got = swap(forward(parts, offsets, left_t, last=True), "fsdp", 1)
    keep = keep_left(place, right_t, grads[-1], toks[-1], left_t)

    cuts = [0, feats // 4, 3 * feats // 4, feats]

    def work(sends, i):
        nonlocal delta
        delta = gradient(place, after(delta, *sends), grads, toks, cuts[i], cuts[i + 1])
        return delta

    mine, other = left_total(place, keep, got, work)
    masks = [(2 << b) - 1 for b in range(replicas.bit_length() - 1)]
    orders = list(zip(masks, masks[::-1]))
    last = len(orders) - 1

    def exchange(bands, step):
        return [swap(x, "rep", m) for x, m in zip(bands, orders[step])]

    y_a = project(place, delta, mine, 0, scale)
    y_b = None
    for t in range(last + 1):
        got_a = exchange(y_a, t)
        if t == 0:
            y_b = project(place, delta, after(other, *y_a), 1, scale)
        got_b = exchange(y_b, t)
        if t == 0:
            inverse = factorize(place, after(mine, *y_b), other, scale)
            *got, inverse = lax.optimization_barrier((*got_a, *got_b, inverse))
            got_a, got_b = got[:2], got[2:]
        if t < last:
            y_a = add_pairs(place, y_a, got_a)
            y_b = add_pairs(place, y_b, got_b)
    basis_cat = make_basis(place, after(mine, *y_a, *y_b), other, inverse, scale)
    common = inverse, basis_cat, delta, momentum, weight, replicas
    *done, rn_t = finish(place, y_a, got_a, *common, 0, None)
    *got_b, rn_t = lax.optimization_barrier((*got_b, rn_t))
    feedback_next, momentum_next, weight_next, rn_t = finish(
        place, y_b, got_b, *common, 1, (*done, rn_t)
    )
    return (feedback_next[None], momentum_next, weight_next, jnp.swapaxes(rn_t, 1, 2))


def solution(mesh):
    placed = (
        P("rep", "fsdp", None),
        P("rep", "fsdp", None),
        P(None, "fsdp", None),
        P("rep", None, "fsdp", None),
        P(None, "fsdp", "rep"),
        P(None, "fsdp", None),
    )
    return jax.shard_map(
        per_device,
        mesh=mesh,
        in_specs=placed,
        out_specs=(
            P("rep", None, "fsdp", None),
            P(None, "fsdp", "rep"),
            P(None, "fsdp", "rep"),
            P(None, "fsdp", None),
        ),
        check_vma=False,
    )
```

```python
import jax
import jax.numpy as jnp
from jax import lax
from jax.experimental import pallas as pl
from jax.experimental.pallas import tpu as pltpu
from jax.sharding import PartitionSpec as P

momentum_decay = 0.9
step_rate = 0.05
highest = lax.Precision.HIGHEST
f32 = jnp.float32
bf16 = jnp.bfloat16
contract_last = (((1,), (1,)), ((), ()))
MIB = 1024 * 1024
vmem = pl.BlockSpec(memory_space=pltpu.VMEM)
smem = pl.BlockSpec(memory_space=pltpu.SMEM)
anywhere = pl.BlockSpec(memory_space=pl.ANY)
hbm = pl.BlockSpec(memory_space=pltpu.HBM)


def kept(like):
    return pltpu.VMEM(like.shape, like.dtype)


def in_vmem(x):
    return pltpu.with_memory_space_constraint(x, pltpu.VMEM)


def in_hbm(x):
    return pltpu.with_memory_space_constraint(x, pltpu.HBM)


def split2(x):
    hi = x.astype(bf16)
    return hi, (x - hi.astype(f32)).astype(bf16)


def stacked(x):
    return jnp.concatenate(split2(x), 0)


def fold(x):
    half = x.shape[0] // 2
    return x[:half] + x[half:]


def dot(a, b):
    return jnp.dot(a, b, preferred_element_type=f32)


def dot_nt(a, b):
    return lax.dot_general(a, b, contract_last, preferred_element_type=f32)


def shape(*dims, dtype=f32):
    return jax.ShapeDtypeStruct(dims, dtype)


def call(body, place, operands, out_shape, mib, macs=0, **more):
    nbytes = sum(x.size * x.dtype.itemsize for x in operands)
    spec = dict(
        in_specs=[smem] + [vmem] * len(operands),
        out_specs=jax.tree.map(lambda _: vmem, out_shape),
    ) | more
    return pl.pallas_call(
        body,
        out_shape=out_shape,
        compiler_params=pltpu.CompilerParams(vmem_limit_bytes=mib * MIB),
        cost_estimate=pl.CostEstimate(flops=2 * macs, bytes_accessed=nbytes, transcendentals=0),
        **spec,
    )(place, *operands)


def divisor(size, most, unit):
    return max(b for b in range(unit, min(size, most) + 1, unit) if size % b == 0)


def span(i, size):
    return pl.ds(pl.multiple_of(i * size, size), size)


def grant(total, feats):
    return 14 if total * feats <= 4 * MIB else 28


def feedback_left(place, feedback, right_t):
    _, rows, feats = feedback.shape
    rank = right_t.shape[1]
    block = 512
    steps = feats // block

    def body(place_ref, fb_ref, r_ref, held_ref, out_ref, sems):
        def copy(k, d):
            cols = slice(d * block, (d + 1) * block)
            return pltpu.make_async_copy(
                fb_ref.at[k, :, cols], held_ref.at[k, :, cols], sems.at[k, d]
            )

        order = [(k, d) for k in range(2) for d in range(steps)]
        for k, d in order:
            copy(k, d).start()
        for k, d in order:
            cols = slice(d * block, (d + 1) * block)
            r_cat = stacked(r_ref[k])
            copy(k, d).wait()
            fb_hi, fb_lo = split2(held_ref[k, :, cols])
            out_ref[k, :, cols] = fold(dot(r_cat, fb_hi)) + dot(r_cat[:rank], fb_lo)

    return call(
        body, place, (in_hbm(feedback), right_t), [kept(feedback), shape(2, rank, feats)], 10,
        2 * rows * feats * 256, name="feedback_left", in_specs=[smem, hbm, vmem],
        scratch_shapes=[pltpu.SemaphoreType.DMA((2, steps))],
    )


def left_part(right, grad, tok):
    return fold(dot(stacked(fold(dot(stacked(right), grad))), tok))


def forward_chunk(place, parts, offsets, weight, upstream, right_t, left_in, last=False):
    count = len(parts)
    feats = parts[0].shape[1]
    width = sum(p.shape[0] for p in parts)
    per = width // len(offsets)
    rows = weight.shape[1]
    rank = right_t.shape[1]

    def body(place_ref, *refs):
        tok_refs, refs = refs[:count], refs[count:]
        w_ref, up_ref, r_ref, left_ref, grad_ref, tok_ref, left_out = refs
        me = place_ref[0]
        at = 0
        for t in tok_refs:
            tok_ref[at : at + t.shape[0], :] = t[...]
            at += t.shape[0]
        gate_pre = dot_nt(w_ref[0], tok_ref[...])
        up_pre = dot_nt(w_ref[1], tok_ref[...])
        cot = jnp.concatenate([up_ref[:, span(me ^ o, per)] for o in offsets], 1).astype(f32)
        s = jax.nn.sigmoid(gate_pre)
        cot_s = cot * s
        grad_ref[0] = (cot_s * up_pre * (1.0 + gate_pre * (1.0 - s))).astype(bf16)
        grad_ref[1] = (cot_s * gate_pre).astype(bf16)
        if last:
            k = (me & 1) ^ 1
            left_out[...] = left_ref[k] + left_part(r_ref[k], grad_ref[k], tok_ref[...])
        else:
            for k in range(2):
                left_out[k] = left_ref[k] + left_part(r_ref[k], grad_ref[k], tok_ref[...])

    return call(
        body, place, (*parts, weight, upstream, right_t, left_in),
        [
            shape(2, rows, width, dtype=bf16), shape(width, feats, dtype=bf16),
            shape(rank, feats) if last else shape(2, rank, feats),
        ],
        grant(width, feats), 2 * rows * feats * width, name="forward_chunk",
    )


def keep_left(place, right_t, grad, tok, left_in):
    _, rank, feats = left_in.shape

    def body(place_ref, r_ref, g_ref, t_ref, left_ref, out_ref):
        k = place_ref[0] & 1
        out_ref[...] = left_ref[k] + left_part(r_ref[k], g_ref[k], t_ref[...])

    return call(
        body, place, (right_t, grad, tok, left_in), shape(rank, feats), 8,
        grad.size * rank, name="keep_left",
    )


def gradient(place, delta, grads, toks, start, stop):
    _, rows, feats = delta.shape
    total = sum(t.shape[0] for t in toks)
    block = 256
    count = len(toks)

    def body(place_ref, fb_ref, *refs):
        for at in range(start, stop, block):
            cols = slice(at, at + block)
            for k in range(2):
                acc = fb_ref[k, :, cols]
                for g, t in zip(refs[:count], refs[count : 2 * count]):
                    acc = acc + dot(g[k], t[:, cols])
                refs[2 * count][k, :, cols] = acc

    return call(
        body, place, (in_vmem(delta), *grads, *toks), kept(delta),
        min(8, grant(total // 2, feats)), 2 * rows * (stop - start) * total,
        name="gradient", input_output_aliases={1: 0},
    )


def project(place, delta, left_t, flip, scale):
    _, rows, feats = delta.shape
    rank = left_t.shape[0]
    block = 512

    def body(place_ref, delta_ref, left_ref, *outs):
        k = (place_ref[0] & 1) ^ flip
        acc = None
        for d in range(feats // block):
            cols = slice(d * block, (d + 1) * block)
            cat = stacked(left_ref[:, cols] * scale)
            hi, lo = split2(delta_ref[k, :, cols])
            part = fold(dot_nt(cat, hi)) + dot_nt(cat[:rank], lo)
            acc = part if acc is None else acc + part
        outs[0][...] = acc[: rank // 2]
        outs[1][...] = acc[rank // 2 :]

    return call(
        body, place, (in_vmem(delta), left_t), [shape(rank // 2, rows)] * 2, 8, rows * feats * 256,
        name="project",
    )


def factorize(place, mine, other, scale):
    rank, feats = mine.shape

    def body(place_ref, mine_ref, other_ref, inv_ref):
        core = place_ref[0] & 1
        row_id = lax.broadcasted_iota(jnp.int32, (rank, 2 * rank), 0)
        eye = (
            lax.broadcasted_iota(jnp.int32, (rank, rank), 0)
            == lax.broadcasted_iota(jnp.int32, (rank, rank), 1)
        ).astype(f32)
        work, roots = [], []
        for k in range(2):
            x = jnp.where(core == k, mine_ref[...], other_ref[...]) * scale
            gram = lax.dot_general(x, x, contract_last, precision=highest, preferred_element_type=f32)
            work.append(jnp.concatenate([gram, eye], 1))
            roots.append(jnp.zeros((rank, 2 * rank), f32))
        group = 8
        for first in range(0, rank, group):
            for k in range(2):
                a = work[k]
                columns = [
                    jnp.broadcast_to(a[:, j : j + 1], a.shape) for j in range(first, first + group)
                ]
                for t in range(group):
                    j = first + t
                    pivot = columns[t][j : j + 1, :]
                    ratio = jnp.where(row_id > j, columns[t] * (1.0 / pivot), 0.0)
                    for u in range(t + 1, group):
                        columns[u] = columns[u] - ratio * columns[u][j : j + 1, :]
                    roots[k] = jnp.where(row_id == j, lax.rsqrt(pivot), roots[k])
                    a = a - ratio * a[j : j + 1, :]
                work[k] = a
        for k in range(2):
            inv_ref[k] = (work[k] * roots[k])[:, rank:]

    return call(
        body, place, (mine, other), shape(2, rank, rank), 8, 1000000, name="factorize"
    )


def make_basis(place, mine, other, inverse, scale):
    rank, feats = mine.shape

    def body(place_ref, mine_ref, other_ref, inv_ref, cat_ref):
        core = place_ref[0] & 1
        for k in range(2):
            x = jnp.where(core == k, mine_ref[...], other_ref[...]) * scale
            basis = jnp.dot(inv_ref[k], x, precision=highest, preferred_element_type=f32)
            b_hi, b_lo = split2(basis)
            cat_ref[k] = jnp.concatenate([b_hi, b_lo, b_hi], 0)

    return call(
        body, place, (mine, other, inverse), shape(2, 3 * rank, feats, dtype=bf16), 8, 1000000,
        name="make_basis",
    )


def finish(place, ys, gots, inverse, basis_cat, delta, momentum, weight, replicas, flip, outs):
    _, rows, feats = delta.shape
    rank = inverse.shape[1]
    cols = momentum.shape[2]
    block = divisor(rows, 128, 16)
    steps = rows // block
    slots = min(4, steps)
    held = () if outs is None else tuple(outs)

    def body(
        place_ref, y0_ref, y1_ref, got0_ref, got1_ref, inv_ref, cat_ref, delta_ref, mom_ref, w_ref, *refs
    ):
        fb_out, mom_out, w_out, rn_out = refs[len(held) : len(held) + 4]
        rn_t, rn_cat, fb_slot, mom_slot, w_slot, sems, rn_sem = refs[len(held) + 4 :]
        slab = span(place_ref[1], cols)
        k = (place_ref[0] & 1) ^ flip
        mean = jnp.concatenate([y0_ref[...] + got0_ref[...], y1_ref[...] + got1_ref[...]], 0)
        rn_t[...] = jnp.dot(
            inv_ref[k], mean * (1.0 / replicas), precision=highest, preferred_element_type=f32
        )
        rn_copy = pltpu.make_async_copy(rn_t, rn_out.at[k], rn_sem)
        rn_copy.start()
        hi, lo = split2(rn_t[...].T)
        rn_cat[...] = jnp.concatenate([hi, hi, lo], 1)

        def copies(i):
            at, slot = slice(i * block, (i + 1) * block), i % slots
            return [
                pltpu.make_async_copy(src.at[slot], dst.at[k, at, :], sems.at[j, slot])
                for j, (src, dst) in enumerate(
                    ((fb_slot, fb_out), (mom_slot, mom_out), (w_slot, w_out))
                )
            ]

        for i in range(steps):
            at, slot = slice(i * block, (i + 1) * block), i % slots
            if i >= slots:
                for c in copies(i - slots):
                    c.wait()
            part = rn_cat[at, :]
            fb_slot[slot] = delta_ref[k, at, :] - dot(part, cat_ref[k])
            mom = momentum_decay * mom_ref[k, at, :] + dot(part, cat_ref[k, :, slab])
            mom_slot[slot] = mom
            w_slot[slot] = (w_ref[k, at, slab].astype(f32) - step_rate * mom).astype(bf16)
            for c in copies(i):
                c.start()
        for i in range(steps - slots, steps):
            for c in copies(i):
                c.wait()
        rn_copy.wait()

    operands = (*ys, *gots, inverse, basis_cat, in_vmem(delta), momentum, weight)
    return call(
        body, place, (*operands, *held),
        [
            shape(2, rows, feats), shape(2, rows, cols),
            shape(2, rows, cols, dtype=bf16), shape(2, rank, rows),
        ],
        10, rows * feats * 256, name="finish",
        in_specs=[smem] + [vmem] * len(operands) + [hbm] * len(held),
        out_specs=[hbm] * 4,
        input_output_aliases={1 + len(operands) + i: i for i in range(len(held))},
        scratch_shapes=[
            pltpu.VMEM((rank, rows), f32),
            pltpu.VMEM((rows, 3 * rank), bf16),
            pltpu.VMEM((slots, block, feats), f32),
            pltpu.VMEM((slots, block, cols), f32),
            pltpu.VMEM((slots, block, cols), bf16),
            pltpu.SemaphoreType.DMA((3, slots)),
            pltpu.SemaphoreType.DMA,
        ],
    )


def swap(x, axis, mask):
    size = lax.axis_size(axis)
    return lax.ppermute(x, axis, [(i, i ^ mask) for i in range(size)])


def after(x, *others):
    return lax.optimization_barrier((x, *others))[0]


def has(place_ref, mask):
    return (place_ref[0] & mask) != 0


def tree(terms):
    while len(terms) > 1:
        terms = [a + b for a, b in zip(terms[::2], terms[1::2])]
    return terms[0]


def add(place, terms):
    def body(place_ref, *refs):
        refs[-1][...] = tree([r[...] for r in refs[:-1]])

    return call(body, place, terms, shape(*terms[0].shape), 4, name="add")


def add_pairs(place, ours, gots):
    count = len(ours)

    def body(place_ref, *refs):
        for j in range(count):
            refs[2 * count + j][...] = refs[j][...] + refs[count + j][...]

    out = [shape(*x.shape) for x in ours]
    return call(body, place, (*ours, *gots), out, 4, name="add_pairs")


def part_of(place_ref, mask=0):
    return (place_ref[0] ^ mask) // 2


def add_cores(place, keep, got, parts):
    rank, feats = keep.shape
    width = feats // parts

    def body(place_ref, keep_ref, got_ref, *outs):
        for m, out in enumerate(outs):
            cols = span(part_of(place_ref, 2 * m), width)
            out[...] = keep_ref[:, cols] + got_ref[:, cols]

    return call(body, place, (keep, got), [shape(rank, width)] * parts, 4, name="add_cores")


def join(place, pieces):
    rank, width = pieces[0].shape

    def body(place_ref, *refs):
        for m, piece in enumerate(refs[:-1]):
            refs[-1][:, span(part_of(place_ref, 2 * m), width)] = piece[...]

    return call(body, place, pieces, shape(rank, width * len(pieces)), 4, name="join")


def left_total(place, keep, got, work):
    fsdp, rep = lax.axis_size("fsdp"), lax.axis_size("rep")
    parts = fsdp // 2

    def beside(sends, axis, masks, i):
        got = [swap(x, axis, m) for x, m in zip(sends, masks)]
        return list(lax.optimization_barrier((*got, work(sends, i)))[:-1])

    far = range(2, fsdp, 2)
    mine, *sends = add_cores(place, keep, got, parts)
    mine = add(place, [mine] + beside(sends, "fsdp", far, 0))
    mine = add(place, [mine] + beside([mine] * (rep - 1), "rep", range(1, rep), 1))
    mine = join(place, [mine] + beside([mine] * (parts - 1), "fsdp", far, 2))
    return mine, swap(mine, "fsdp", 1)


def per_device(tokens, upstream, weight, feedback, momentum, right_factor):
    fsdp, replicas = lax.axis_size("fsdp"), lax.axis_size("rep")
    place = jnp.stack([lax.axis_index("fsdp"), lax.axis_index("rep")]).astype(jnp.int32)
    own = tokens[0]
    per, feats = own.shape
    inner = [1 << b for b in range(fsdp.bit_length() - 3)]
    far_x, far_y = fsdp // 4, fsdp // 2
    right_t = jnp.swapaxes(right_factor, 1, 2)
    scale = 1.0 / replicas

    def gather_inner(parts, base):
        parts, offsets = list(parts), [base]
        for m in inner:
            parts = parts + [swap(p, "fsdp", m) for p in parts]
            offsets = offsets + [o ^ m for o in offsets]
        return parts, offsets

    def halves(x, y):
        def body(place_ref, x_ref, y_ref, x_out, y_out):
            x_out[...] = x_ref[: per // 2, :]
            y_out[...] = y_ref[per // 2 :, :]

        return call(body, place, (x, y), [shape(per // 2, feats, dtype=bf16)] * 2, 4, name="halves")

    grads, toks = [], []

    def forward(parts, offsets, left, last=False):
        grad, tok, left = forward_chunk(
            place, parts, offsets, weight, upstream[0], right_t, left, last
        )
        grads.append(grad)
        toks.append(tok)
        return left

    got_x = swap(own, "fsdp", far_x)
    got_y = swap(own, "fsdp", far_y)
    parts, offsets = gather_inner([own], 0)
    delta, left_t = feedback_left(place, feedback[0], right_t)
    left_t = forward(parts, offsets, left_t)
    got_x, got_y, left_t = lax.optimization_barrier((got_x, got_y, left_t))
    send_x, send_y = halves(got_x, got_y)
    far = [swap(send_x, "fsdp", far_y), swap(send_y, "fsdp", far_x)]
    parts_x, offsets_x = gather_inner([got_x], far_x)
    parts_y, offsets_y = gather_inner([got_y], far_y)
    left_t = forward(parts_x + parts_y, offsets_x + offsets_y, left_t)
    far_0, far_1, left_t = lax.optimization_barrier((*far, left_t))
    parts, offsets = gather_inner([far_0, far_1], far_x ^ far_y)
    got = swap(forward(parts, offsets, left_t, last=True), "fsdp", 1)
    keep = keep_left(place, right_t, grads[-1], toks[-1], left_t)

    cuts = [0, feats // 4, 3 * feats // 4, feats]

    def work(sends, i):
        nonlocal delta
        delta = gradient(place, after(delta, *sends), grads, toks, cuts[i], cuts[i + 1])
        return delta

    mine, other = left_total(place, keep, got, work)
    masks = [(2 << b) - 1 for b in range(replicas.bit_length() - 1)]
    orders = list(zip(masks, masks[::-1]))
    last = len(orders) - 1

    def exchange(bands, step):
        return [swap(x, "rep", m) for x, m in zip(bands, orders[step])]

    y_a = project(place, delta, mine, 0, scale)
    got_a = exchange(y_a, 0)
    y_b = project(place, delta, after(other, *y_a), 1, scale)
    got_b = exchange(y_b, 0)
    *got_a, _ = lax.optimization_barrier((*got_a, y_b[0]))
    for t in range(last):
        y_a = add_pairs(place, y_a, got_a)
        got_a = exchange(y_a, t + 1)
    inverse = factorize(place, after(mine, *y_a), other, scale)
    *got_b, inverse = lax.optimization_barrier((*got_b, inverse))
    for t in range(last):
        y_b = add_pairs(place, y_b, got_b)
        got_b = exchange(y_b, t + 1)
    basis_cat = make_basis(place, after(mine, *y_a, *y_b), other, inverse, scale)
    common = inverse, basis_cat, delta, momentum, weight, replicas
    *done, rn_t = finish(place, y_a, got_a, *common, 0, None)
    *got_b, rn_t = lax.optimization_barrier((*got_b, rn_t))
    feedback_next, momentum_next, weight_next, rn_t = finish(
        place, y_b, got_b, *common, 1, (*done, rn_t)
    )
    return (feedback_next[None], momentum_next, weight_next, jnp.swapaxes(rn_t, 1, 2))


def solution(mesh):
    placed = (
        P("rep", "fsdp", None),
        P("rep", "fsdp", None),
        P(None, "fsdp", None),
        P("rep", None, "fsdp", None),
        P(None, "fsdp", "rep"),
        P(None, "fsdp", None),
    )
    return jax.shard_map(
        per_device,
        mesh=mesh,
        in_specs=placed,
        out_specs=(
            P("rep", None, "fsdp", None),
            P(None, "fsdp", "rep"),
            P(None, "fsdp", "rep"),
            P(None, "fsdp", None),
        ),
        check_vma=False,
    )
```

```python
import jax
import jax.numpy as jnp
from jax import lax
from jax.experimental import pallas as pl
from jax.experimental.pallas import tpu as pltpu
from jax.sharding import PartitionSpec as P

momentum_decay = 0.9
step_rate = 0.05
f32 = jnp.float32
bf16 = jnp.bfloat16
contract_last = (((1,), (1,)), ((), ()))
MIB = 1024 * 1024
vmem = pl.BlockSpec(memory_space=pltpu.VMEM)
smem = pl.BlockSpec(memory_space=pltpu.SMEM)
anywhere = pl.BlockSpec(memory_space=pl.ANY)
hbm = pl.BlockSpec(memory_space=pltpu.HBM)


def kept(like):
    return pltpu.VMEM(like.shape, like.dtype)


def in_vmem(x):
    return pltpu.with_memory_space_constraint(x, pltpu.VMEM)


def in_hbm(x):
    return pltpu.with_memory_space_constraint(x, pltpu.HBM)


def split2(x):
    hi = x.astype(bf16)
    return hi, (x - hi.astype(f32)).astype(bf16)


def split3(x):
    hi = x.astype(bf16)
    rest = x - hi.astype(f32)
    mid = rest.astype(bf16)
    return hi, mid, (rest - mid.astype(f32)).astype(bf16)


def dot_full(a, b):
    h, m, l = split3(a)
    p, q, r = split3(b)
    return dot(jnp.concatenate([h, h, m, h, m, l], 1), jnp.concatenate([p, q, p, r, q, p], 0))


def gram_full(x):
    n = x.shape[0]
    parts = jnp.concatenate(split3(x), 0)
    blocks = dot_nt(parts, parts)
    total = None
    for order in (4, 3, 2, 1, 0):
        for i in range(3):
            if 0 <= order - i <= 2:
                j = order - i
                block = blocks[i * n : (i + 1) * n, j * n : (j + 1) * n]
                total = block if total is None else total + block
    return total


def stacked(x):
    return jnp.concatenate(split2(x), 0)


def fold(x):
    half = x.shape[0] // 2
    return x[:half] + x[half:]


def dot(a, b):
    return jnp.dot(a, b, preferred_element_type=f32)


def dot_nt(a, b):
    return lax.dot_general(a, b, contract_last, preferred_element_type=f32)


def shape(*dims, dtype=f32):
    return jax.ShapeDtypeStruct(dims, dtype)


def call(body, place, operands, out_shape, mib, macs=0, **more):
    nbytes = sum(x.size * x.dtype.itemsize for x in operands)
    spec = dict(
        in_specs=[smem] + [vmem] * len(operands),
        out_specs=jax.tree.map(lambda _: vmem, out_shape),
    ) | more
    return pl.pallas_call(
        body,
        out_shape=out_shape,
        compiler_params=pltpu.CompilerParams(vmem_limit_bytes=mib * MIB),
        cost_estimate=pl.CostEstimate(flops=2 * macs, bytes_accessed=nbytes, transcendentals=0),
        **spec,
    )(place, *operands)


def divisor(size, most, unit):
    return max(b for b in range(unit, min(size, most) + 1, unit) if size % b == 0)


def span(i, size):
    return pl.ds(pl.multiple_of(i * size, size), size)


def grant(total, feats):
    return 14 if total * feats <= 4 * MIB else 28


def feedback_left(place, feedback, right_t):
    _, rows, feats = feedback.shape
    rank = right_t.shape[1]
    block = 512
    steps = feats // block

    def body(place_ref, fb_ref, r_ref, held_ref, out_ref, sems):
        def copy(k, d):
            cols = slice(d * block, (d + 1) * block)
            return pltpu.make_async_copy(
                fb_ref.at[k, :, cols], held_ref.at[k, :, cols], sems.at[k, d]
            )

        order = [(k, d) for k in range(2) for d in range(steps)]
        for k, d in order:
            copy(k, d).start()
        for k, d in order:
            cols = slice(d * block, (d + 1) * block)
            r_cat = stacked(r_ref[k])
            copy(k, d).wait()
            fb_hi, fb_lo = split2(held_ref[k, :, cols])
            out_ref[k, :, cols] = fold(dot(r_cat, fb_hi)) + dot(r_cat[:rank], fb_lo)

    return call(
        body, place, (in_hbm(feedback), right_t), [kept(feedback), shape(2, rank, feats)], 10,
        2 * rows * feats * 256, name="feedback_left", in_specs=[smem, hbm, vmem],
        scratch_shapes=[pltpu.SemaphoreType.DMA((2, steps))],
    )


def left_part(right, grad, tok):
    return fold(dot(stacked(fold(dot(stacked(right), grad))), tok))


def forward_chunk(place, parts, offsets, weight, upstream, right_t, left_in, last=False):
    count = len(parts)
    feats = parts[0].shape[1]
    width = sum(p.shape[0] for p in parts)
    per = width // len(offsets)
    rows = weight.shape[1]
    rank = right_t.shape[1]

    def body(place_ref, *refs):
        tok_refs, refs = refs[:count], refs[count:]
        w_ref, up_ref, r_ref, left_ref, grad_ref, tok_ref, left_out = refs
        me = place_ref[0]
        at = 0
        for t in tok_refs:
            tok_ref[at : at + t.shape[0], :] = t[...]
            at += t.shape[0]
        gate_pre = dot_nt(w_ref[0], tok_ref[...])
        up_pre = dot_nt(w_ref[1], tok_ref[...])
        shards = [me ^ (even + (me & 1) * (odd - even)) for even, odd in offsets]
        cot = jnp.concatenate([up_ref[:, span(j, per)] for j in shards], 1).astype(f32)
        s = jax.nn.sigmoid(gate_pre)
        cot_s = cot * s
        grad_ref[0] = (cot_s * up_pre * (1.0 + gate_pre * (1.0 - s))).astype(bf16)
        grad_ref[1] = (cot_s * gate_pre).astype(bf16)
        if last:
            k = (me & 1) ^ 1
            left_out[...] = left_ref[k] + left_part(r_ref[k], grad_ref[k], tok_ref[...])
        else:
            for k in range(2):
                left_out[k] = left_ref[k] + left_part(r_ref[k], grad_ref[k], tok_ref[...])

    return call(
        body, place, (*parts, weight, upstream, right_t, left_in),
        [
            shape(2, rows, width, dtype=bf16), shape(width, feats, dtype=bf16),
            shape(rank, feats) if last else shape(2, rank, feats),
        ],
        grant(width, feats), 2 * rows * feats * width, name="forward_chunk",
    )


def keep_left(place, right_t, grad, tok, left_in):
    _, rank, feats = left_in.shape

    def body(place_ref, r_ref, g_ref, t_ref, left_ref, out_ref):
        k = place_ref[0] & 1
        out_ref[...] = left_ref[k] + left_part(r_ref[k], g_ref[k], t_ref[...])

    return call(
        body, place, (right_t, grad, tok, left_in), shape(rank, feats), 8,
        grad.size * rank, name="keep_left",
    )


def gradient(place, delta, grads, toks, start, stop):
    _, rows, feats = delta.shape
    total = sum(t.shape[0] for t in toks)
    block = 256
    count = len(toks)

    def body(place_ref, fb_ref, *refs):
        for at in range(start, stop, block):
            cols = slice(at, at + block)
            for k in range(2):
                acc = fb_ref[k, :, cols]
                for g, t in zip(refs[:count], refs[count : 2 * count]):
                    acc = acc + dot(g[k], t[:, cols])
                refs[2 * count][k, :, cols] = acc

    return call(
        body, place, (in_vmem(delta), *grads, *toks), kept(delta),
        min(8, grant(total // 2, feats)), 2 * rows * (stop - start) * total,
        name="gradient", input_output_aliases={1: 0},
    )


def project(place, delta, left_t, flip, scale):
    _, rows, feats = delta.shape
    rank = left_t.shape[0]
    block = 512

    def body(place_ref, delta_ref, left_ref, *outs):
        k = (place_ref[0] & 1) ^ flip
        acc = None
        for d in range(feats // block):
            cols = slice(d * block, (d + 1) * block)
            cat = stacked(left_ref[:, cols] * scale)
            hi, lo = split2(delta_ref[k, :, cols])
            part = fold(dot_nt(cat, hi)) + dot_nt(cat[:rank], lo)
            acc = part if acc is None else acc + part
        outs[0][...] = acc[: rank // 2]
        outs[1][...] = acc[rank // 2 :]

    return call(
        body, place, (in_vmem(delta), left_t), [shape(rank // 2, rows)] * 2, 8, rows * feats * 256,
        name="project",
    )


def factorize(place, mine, other, scale):
    rank, feats = mine.shape

    def body(place_ref, mine_ref, other_ref, inv_ref):
        core = place_ref[0] & 1
        row_id = lax.broadcasted_iota(jnp.int32, (rank, 2 * rank), 0)
        eye = (
            lax.broadcasted_iota(jnp.int32, (rank, rank), 0)
            == lax.broadcasted_iota(jnp.int32, (rank, rank), 1)
        ).astype(f32)
        work, roots = [], []
        for k in range(2):
            x = jnp.where(core == k, mine_ref[...], other_ref[...]) * scale
            gram = gram_full(x)
            work.append(jnp.concatenate([gram, eye], 1))
            roots.append(jnp.zeros((rank, 2 * rank), f32))
        group = 8
        for first in range(0, rank, group):
            for k in range(2):
                a = work[k]
                columns = [
                    jnp.broadcast_to(a[:, j : j + 1], a.shape) for j in range(first, first + group)
                ]
                for t in range(group):
                    j = first + t
                    pivot = columns[t][j : j + 1, :]
                    ratio = jnp.where(row_id > j, columns[t] * (1.0 / pivot), 0.0)
                    for u in range(t + 1, group):
                        columns[u] = columns[u] - ratio * columns[u][j : j + 1, :]
                    roots[k] = jnp.where(row_id == j, lax.rsqrt(pivot), roots[k])
                    a = a - ratio * a[j : j + 1, :]
                work[k] = a
        for k in range(2):
            inv_ref[k] = (work[k] * roots[k])[:, rank:]

    return call(
        body, place, (mine, other), shape(2, rank, rank), 8, 1000000, name="factorize"
    )


def make_basis(place, mine, other, inverse, scale):
    rank, feats = mine.shape

    def body(place_ref, mine_ref, other_ref, inv_ref, cat_ref):
        core = place_ref[0] & 1
        for k in range(2):
            x = jnp.where(core == k, mine_ref[...], other_ref[...]) * scale
            basis = dot_full(inv_ref[k], x)
            b_hi, b_lo = split2(basis)
            cat_ref[k] = jnp.concatenate([b_hi, b_lo, b_hi], 0)

    return call(
        body, place, (mine, other, inverse), shape(2, 3 * rank, feats, dtype=bf16), 8, 1000000,
        name="make_basis",
    )


def finish(place, ys, gots, inverse, basis_cat, delta, momentum, weight, replicas, flip, outs):
    _, rows, feats = delta.shape
    rank = inverse.shape[1]
    cols = momentum.shape[2]
    block = divisor(rows, 128, 16)
    steps = rows // block
    slots = min(4, steps)
    held = () if outs is None else tuple(outs)

    def body(
        place_ref, y0_ref, y1_ref, got0_ref, got1_ref, inv_ref, cat_ref, delta_ref, mom_ref, w_ref, *refs
    ):
        fb_out, mom_out, w_out, rn_out = refs[len(held) : len(held) + 4]
        rn_t, rn_cat, fb_slot, mom_slot, w_slot, sems, rn_sem = refs[len(held) + 4 :]
        slab = span(place_ref[1], cols)
        k = (place_ref[0] & 1) ^ flip
        mean = jnp.concatenate([y0_ref[...] + got0_ref[...], y1_ref[...] + got1_ref[...]], 0)
        rn_t[...] = dot_full(inv_ref[k], mean * (1.0 / replicas))
        rn_copy = pltpu.make_async_copy(rn_t, rn_out.at[k], rn_sem)
        rn_copy.start()
        hi, lo = split2(rn_t[...].T)
        rn_cat[...] = jnp.concatenate([hi, hi, lo], 1)

        def copies(i):
            at, slot = slice(i * block, (i + 1) * block), i % slots
            return [
                pltpu.make_async_copy(src.at[slot], dst.at[k, at, :], sems.at[j, slot])
                for j, (src, dst) in enumerate(
                    ((fb_slot, fb_out), (mom_slot, mom_out), (w_slot, w_out))
                )
            ]

        for i in range(steps):
            at, slot = slice(i * block, (i + 1) * block), i % slots
            if i >= slots:
                for c in copies(i - slots):
                    c.wait()
            part = rn_cat[at, :]
            fb_slot[slot] = delta_ref[k, at, :] - dot(part, cat_ref[k])
            mom = momentum_decay * mom_ref[k, at, :] + dot(part, cat_ref[k, :, slab])
            mom_slot[slot] = mom
            w_slot[slot] = (w_ref[k, at, slab].astype(f32) - step_rate * mom).astype(bf16)
            for c in copies(i):
                c.start()
        for i in range(steps - slots, steps):
            for c in copies(i):
                c.wait()
        rn_copy.wait()

    operands = (*ys, *gots, inverse, basis_cat, in_vmem(delta), momentum, weight)
    return call(
        body, place, (*operands, *held),
        [
            shape(2, rows, feats), shape(2, rows, cols),
            shape(2, rows, cols, dtype=bf16), shape(2, rank, rows),
        ],
        10, rows * feats * 256, name="finish",
        in_specs=[smem] + [vmem] * len(operands) + [hbm] * len(held),
        out_specs=[hbm] * 4,
        input_output_aliases={1 + len(operands) + i: i for i in range(len(held))},
        scratch_shapes=[
            pltpu.VMEM((rank, rows), f32),
            pltpu.VMEM((rows, 3 * rank), bf16),
            pltpu.VMEM((slots, block, feats), f32),
            pltpu.VMEM((slots, block, cols), f32),
            pltpu.VMEM((slots, block, cols), bf16),
            pltpu.SemaphoreType.DMA((3, slots)),
            pltpu.SemaphoreType.DMA,
        ],
    )


def swap(x, axis, mask):
    size = lax.axis_size(axis)
    return lax.ppermute(x, axis, [(i, i ^ mask) for i in range(size)])


def after(x, *others):
    return lax.optimization_barrier((x, *others))[0]


def has(place_ref, mask):
    return (place_ref[0] & mask) != 0


def tree(terms):
    while len(terms) > 1:
        terms = [a + b for a, b in zip(terms[::2], terms[1::2])]
    return terms[0]


def add(place, terms):
    def body(place_ref, *refs):
        refs[-1][...] = tree([r[...] for r in refs[:-1]])

    return call(body, place, terms, shape(*terms[0].shape), 4, name="add")


def add_pairs(place, ours, gots):
    count = len(ours)

    def body(place_ref, *refs):
        for j in range(count):
            refs[2 * count + j][...] = refs[j][...] + refs[count + j][...]

    out = [shape(*x.shape) for x in ours]
    return call(body, place, (*ours, *gots), out, 4, name="add_pairs")


def part_of(place_ref, mask=0):
    return (place_ref[0] ^ mask) // 2


def add_cores(place, keep, got, parts):
    rank, feats = keep.shape
    width = feats // parts

    def body(place_ref, keep_ref, got_ref, *outs):
        for m, out in enumerate(outs):
            cols = span(part_of(place_ref, 2 * m), width)
            out[...] = keep_ref[:, cols] + got_ref[:, cols]

    return call(body, place, (keep, got), [shape(rank, width)] * parts, 4, name="add_cores")


def join(place, pieces):
    rank, width = pieces[0].shape

    def body(place_ref, *refs):
        for m, piece in enumerate(refs[:-1]):
            refs[-1][:, span(part_of(place_ref, 2 * m), width)] = piece[...]

    return call(body, place, pieces, shape(rank, width * len(pieces)), 4, name="join")


def left_total(place, keep, got, work):
    fsdp, rep = lax.axis_size("fsdp"), lax.axis_size("rep")
    parts = fsdp // 2

    def beside(sends, axis, masks, i):
        got = [swap(x, axis, m) for x, m in zip(sends, masks)]
        return list(lax.optimization_barrier((*got, work(sends, i)))[:-1])

    far = range(2, fsdp, 2)
    mine, *sends = add_cores(place, keep, got, parts)
    mine = add(place, [mine] + beside(sends, "fsdp", far, 0))
    mine = add(place, [mine] + beside([mine] * (rep - 1), "rep", range(1, rep), 1))
    mine = join(place, [mine] + beside([mine] * (parts - 1), "fsdp", far, 2))
    return mine, swap(mine, "fsdp", 1)


def per_device(tokens, upstream, weight, feedback, momentum, right_factor):
    fsdp, replicas = lax.axis_size("fsdp"), lax.axis_size("rep")
    place = jnp.stack([lax.axis_index("fsdp"), lax.axis_index("rep")]).astype(jnp.int32)
    own = tokens[0]
    per, feats = own.shape
    inner = [1 << b for b in range(fsdp.bit_length() - 3)]
    far_x, far_y = fsdp // 4, fsdp // 2
    right_t = jnp.swapaxes(right_factor, 1, 2)
    scale = 1.0 / replicas

    def gather_inner(part, even_mask, odd_mask):
        parts, inners = [part], [0]
        for m in inner:
            parts = parts + [swap(p, "fsdp", m) for p in parts]
            inners = inners + [o ^ m for o in inners]
        masks = even_mask, odd_mask
        return parts, [(o ^ masks[o & 1], o ^ masks[1 - (o & 1)]) for o in inners]

    def swap_far(x, even_mask, odd_mask):
        masks = even_mask, odd_mask
        return lax.ppermute(x, "fsdp", [(i, i ^ masks[i & 1]) for i in range(fsdp)])

    grads, toks = [], []

    def forward(parts, offsets, left, last=False):
        grad, tok, left = forward_chunk(
            place, parts, offsets, weight, upstream[0], right_t, left, last
        )
        grads.append(grad)
        toks.append(tok)
        return left

    got_1 = swap_far(own, far_x, far_y)
    got_2 = swap_far(own, far_y, far_x)
    chunk_0 = gather_inner(own, 0, 0)
    delta, left_t = feedback_left(place, feedback[0], right_t)
    left_t = forward(*chunk_0, left_t)
    got_1, got_2, left_t = lax.optimization_barrier((got_1, got_2, left_t))
    got_3 = swap_far(got_1, far_y, far_x)
    chunk_1 = gather_inner(got_1, far_x, far_y)
    chunk_2 = gather_inner(got_2, far_y, far_x)
    left_t = forward(chunk_1[0] + chunk_2[0], chunk_1[1] + chunk_2[1], left_t)
    got_3, left_t = lax.optimization_barrier((got_3, left_t))
    chunk_3 = gather_inner(got_3, far_x ^ far_y, far_x ^ far_y)
    got = swap(forward(*chunk_3, left_t, last=True), "fsdp", 1)
    keep = keep_left(place, right_t, grads[-1], toks[-1], left_t)

    cuts = [0, feats // 4, 3 * feats // 4, feats]

    def work(sends, i):
        nonlocal delta
        delta = gradient(place, after(delta, *sends), grads, toks, cuts[i], cuts[i + 1])
        return delta

    mine, other = left_total(place, keep, got, work)
    masks = [(2 << b) - 1 for b in range(replicas.bit_length() - 1)]
    orders = list(zip(masks, masks[::-1]))
    last = len(orders) - 1

    def exchange(bands, step):
        return [swap(x, "rep", m) for x, m in zip(bands, orders[step])]

    y_a = project(place, delta, mine, 0, scale)
    got_a = exchange(y_a, 0)
    y_b = project(place, delta, after(other, *y_a), 1, scale)
    got_b = exchange(y_b, 0)
    *got_a, _ = lax.optimization_barrier((*got_a, y_b[0]))
    for t in range(last):
        y_a = add_pairs(place, y_a, got_a)
        got_a = exchange(y_a, t + 1)
    inverse = factorize(place, after(mine, *y_a), other, scale)
    *got_b, inverse = lax.optimization_barrier((*got_b, inverse))
    for t in range(last):
        y_b = add_pairs(place, y_b, got_b)
        got_b = exchange(y_b, t + 1)
    basis_cat = make_basis(place, after(mine, *y_a, *y_b), other, inverse, scale)
    common = inverse, basis_cat, delta, momentum, weight, replicas
    *done, rn_t = finish(place, y_a, got_a, *common, 0, None)
    *got_b, rn_t = lax.optimization_barrier((*got_b, rn_t))
    feedback_next, momentum_next, weight_next, rn_t = finish(
        place, y_b, got_b, *common, 1, (*done, rn_t)
    )
    return (feedback_next[None], momentum_next, weight_next, jnp.swapaxes(rn_t, 1, 2))


def solution(mesh):
    placed = (
        P("rep", "fsdp", None),
        P("rep", "fsdp", None),
        P(None, "fsdp", None),
        P("rep", None, "fsdp", None),
        P(None, "fsdp", "rep"),
        P(None, "fsdp", None),
    )
    return jax.shard_map(
        per_device,
        mesh=mesh,
        in_specs=placed,
        out_specs=(
            P("rep", None, "fsdp", None),
            P(None, "fsdp", "rep"),
            P(None, "fsdp", "rep"),
            P(None, "fsdp", None),
        ),
        check_vma=False,
    )
```

```python
import jax
import jax.numpy as jnp
from jax import lax
from jax.experimental import pallas as pl
from jax.experimental.pallas import tpu as pltpu
from jax.sharding import PartitionSpec as P

momentum_decay = 0.9
step_rate = 0.05
f32 = jnp.float32
bf16 = jnp.bfloat16
contract_last = (((1,), (1,)), ((), ()))
MIB = 1024 * 1024
vmem = pl.BlockSpec(memory_space=pltpu.VMEM)
smem = pl.BlockSpec(memory_space=pltpu.SMEM)
anywhere = pl.BlockSpec(memory_space=pl.ANY)
hbm = pl.BlockSpec(memory_space=pltpu.HBM)


def kept(like):
    return pltpu.VMEM(like.shape, like.dtype)


def in_vmem(x):
    return pltpu.with_memory_space_constraint(x, pltpu.VMEM)


def in_hbm(x):
    return pltpu.with_memory_space_constraint(x, pltpu.HBM)


def split2(x):
    hi = x.astype(bf16)
    return hi, (x - hi.astype(f32)).astype(bf16)


def split3(x):
    hi = x.astype(bf16)
    rest = x - hi.astype(f32)
    mid = rest.astype(bf16)
    return hi, mid, (rest - mid.astype(f32)).astype(bf16)


def dot_full(a, b):
    h, m, l = split3(a)
    p, q, r = split3(b)
    return dot(jnp.concatenate([h, h, m, h, m, l], 1), jnp.concatenate([p, q, p, r, q, p], 0))


def gram_full(x):
    n = x.shape[0]
    parts = jnp.concatenate(split3(x), 0)
    blocks = dot_nt(parts, parts)
    total = None
    for order in (4, 3, 2, 1, 0):
        for i in range(3):
            if 0 <= order - i <= 2:
                j = order - i
                block = blocks[i * n : (i + 1) * n, j * n : (j + 1) * n]
                total = block if total is None else total + block
    return total


def stacked(x):
    return jnp.concatenate(split2(x), 0)


def fold(x):
    half = x.shape[0] // 2
    return x[:half] + x[half:]


def dot(a, b):
    return jnp.dot(a, b, preferred_element_type=f32)


def dot_nt(a, b):
    return lax.dot_general(a, b, contract_last, preferred_element_type=f32)


def shape(*dims, dtype=f32):
    return jax.ShapeDtypeStruct(dims, dtype)


def call(body, place, operands, out_shape, mib, macs=0, **more):
    nbytes = sum(x.size * x.dtype.itemsize for x in operands)
    spec = dict(
        in_specs=[smem] + [vmem] * len(operands),
        out_specs=jax.tree.map(lambda _: vmem, out_shape),
    ) | more
    return pl.pallas_call(
        body,
        out_shape=out_shape,
        compiler_params=pltpu.CompilerParams(vmem_limit_bytes=mib * MIB),
        cost_estimate=pl.CostEstimate(flops=2 * macs, bytes_accessed=nbytes, transcendentals=0),
        **spec,
    )(place, *operands)


def divisor(size, most, unit):
    return max(b for b in range(unit, min(size, most) + 1, unit) if size % b == 0)


def span(i, size):
    return pl.ds(pl.multiple_of(i * size, size), size)


def grant(total, feats):
    return 14 if total * feats <= 4 * MIB else 28


def feedback_left(place, feedback, right_t):
    _, rows, feats = feedback.shape
    rank = right_t.shape[1]
    block = 512
    steps = feats // block

    def body(place_ref, fb_ref, r_ref, held_ref, out_ref, right, sems, right_sem):
        right_copy = pltpu.make_async_copy(r_ref, right, right_sem)
        right_copy.start()

        def copy(k, d):
            cols = slice(d * block, (d + 1) * block)
            return pltpu.make_async_copy(
                fb_ref.at[k, :, cols], held_ref.at[k, :, cols], sems.at[k, d]
            )

        order = [(k, d) for k in range(2) for d in range(steps)]
        for k, d in order:
            copy(k, d).start()
        right_copy.wait()
        for k, d in order:
            cols = slice(d * block, (d + 1) * block)
            r_cat = stacked(right[k])
            copy(k, d).wait()
            fb_hi, fb_lo = split2(held_ref[k, :, cols])
            out_ref[k, :, cols] = fold(dot(r_cat, fb_hi)) + dot(r_cat[:rank], fb_lo)

    return call(
        body, place, (in_hbm(feedback), in_hbm(right_t)), [kept(feedback), shape(2, rank, feats)], 10,
        2 * rows * feats * 256, name="feedback_left", in_specs=[smem, hbm, hbm],
        scratch_shapes=[
            pltpu.VMEM((2, rank, rows), f32),
            pltpu.SemaphoreType.DMA((2, steps)),
            pltpu.SemaphoreType.DMA,
        ],
    )


def left_part(right, grad, tok):
    return fold(dot(stacked(fold(dot(stacked(right), grad))), tok))


def forward_chunk(place, parts, offsets, weight, upstream, right_t, left_in, last=False):
    count = len(parts)
    feats = parts[0].shape[1]
    width = sum(p.shape[0] for p in parts)
    per = width // len(offsets)
    rows = weight.shape[1]
    rank = right_t.shape[1]

    def body(place_ref, *refs):
        tok_refs, refs = refs[:count], refs[count:]
        w_ref, up_ref, r_ref, left_ref, grad_ref, tok_ref, left_out = refs
        me = place_ref[0]
        at = 0
        for t in tok_refs:
            tok_ref[at : at + t.shape[0], :] = t[...]
            at += t.shape[0]
        gate_pre = dot_nt(w_ref[0], tok_ref[...])
        up_pre = dot_nt(w_ref[1], tok_ref[...])
        shards = [me ^ (even + (me & 1) * (odd - even)) for even, odd in offsets]
        cot = jnp.concatenate([up_ref[:, span(j, per)] for j in shards], 1).astype(f32)
        s = jax.nn.sigmoid(gate_pre)
        cot_s = cot * s
        grad_ref[0] = (cot_s * up_pre * (1.0 + gate_pre * (1.0 - s))).astype(bf16)
        grad_ref[1] = (cot_s * gate_pre).astype(bf16)
        if last:
            k = (me & 1) ^ 1
            left_out[...] = left_ref[k] + left_part(r_ref[k], grad_ref[k], tok_ref[...])
        else:
            for k in range(2):
                left_out[k] = left_ref[k] + left_part(r_ref[k], grad_ref[k], tok_ref[...])

    return call(
        body, place, (*parts, weight, upstream, right_t, left_in),
        [
            shape(2, rows, width, dtype=bf16), shape(width, feats, dtype=bf16),
            shape(rank, feats) if last else shape(2, rank, feats),
        ],
        grant(width, feats), 2 * rows * feats * width, name="forward_chunk",
    )


def keep_left(place, right_t, grad, tok, left_in):
    _, rank, feats = left_in.shape

    def body(place_ref, r_ref, g_ref, t_ref, left_ref, out_ref):
        k = place_ref[0] & 1
        out_ref[...] = left_ref[k] + left_part(r_ref[k], g_ref[k], t_ref[...])

    return call(
        body, place, (right_t, grad, tok, left_in), shape(rank, feats), 8,
        grad.size * rank, name="keep_left",
    )


def gradient(place, delta, grads, toks, start, stop):
    _, rows, feats = delta.shape
    total = sum(t.shape[0] for t in toks)
    block = 256
    count = len(toks)

    def body(place_ref, fb_ref, *refs):
        for at in range(start, stop, block):
            cols = slice(at, at + block)
            for k in range(2):
                acc = fb_ref[k, :, cols]
                for g, t in zip(refs[:count], refs[count : 2 * count]):
                    acc = acc + dot(g[k], t[:, cols])
                refs[2 * count][k, :, cols] = acc

    return call(
        body, place, (in_vmem(delta), *grads, *toks), kept(delta),
        min(8, grant(total // 2, feats)), 2 * rows * (stop - start) * total,
        name="gradient", input_output_aliases={1: 0},
    )


def project(place, delta, left_t, flip, scale):
    _, rows, feats = delta.shape
    rank = left_t.shape[0]
    block = 512

    def body(place_ref, delta_ref, left_ref, *outs):
        k = (place_ref[0] & 1) ^ flip
        acc = None
        for d in range(feats // block):
            cols = slice(d * block, (d + 1) * block)
            cat = stacked(left_ref[:, cols] * scale)
            hi, lo = split2(delta_ref[k, :, cols])
            part = fold(dot_nt(cat, hi)) + dot_nt(cat[:rank], lo)
            acc = part if acc is None else acc + part
        outs[0][...] = acc[: rank // 2]
        outs[1][...] = acc[rank // 2 :]

    return call(
        body, place, (in_vmem(delta), left_t), [shape(rank // 2, rows)] * 2, 8, rows * feats * 256,
        name="project",
    )


def factorize(place, mine, other, scale):
    rank, feats = mine.shape

    def body(place_ref, mine_ref, other_ref, inv_ref, cat_ref):
        core = place_ref[0] & 1
        row_id = lax.broadcasted_iota(jnp.int32, (rank, 2 * rank), 0)
        eye = (
            lax.broadcasted_iota(jnp.int32, (rank, rank), 0)
            == lax.broadcasted_iota(jnp.int32, (rank, rank), 1)
        ).astype(f32)
        lefts, work, roots = [], [], []
        for k in range(2):
            x = jnp.where(core == k, mine_ref[...], other_ref[...]) * scale
            gram = gram_full(x)
            lefts.append(x)
            work.append(jnp.concatenate([gram, eye], 1))
            roots.append(jnp.zeros((rank, 2 * rank), f32))
        group = 8
        for first in range(0, rank, group):
            for k in range(2):
                a = work[k]
                columns = [
                    jnp.broadcast_to(a[:, j : j + 1], a.shape) for j in range(first, first + group)
                ]
                for t in range(group):
                    j = first + t
                    pivot = columns[t][j : j + 1, :]
                    ratio = jnp.where(row_id > j, columns[t] * (1.0 / pivot), 0.0)
                    for u in range(t + 1, group):
                        columns[u] = columns[u] - ratio * columns[u][j : j + 1, :]
                    roots[k] = jnp.where(row_id == j, lax.rsqrt(pivot), roots[k])
                    a = a - ratio * a[j : j + 1, :]
                work[k] = a
        for k in range(2):
            inv = (work[k] * roots[k])[:, rank:]
            inv_ref[k] = inv
            b_hi, b_lo = split2(dot_full(inv, lefts[k]))
            cat_ref[k] = jnp.concatenate([b_hi, b_lo, b_hi], 0)

    return call(
        body, place, (mine, other),
        [shape(2, rank, rank), shape(2, 3 * rank, feats, dtype=bf16)], 12, 1000000, name="factorize",
    )


def finish(place, ys, gots, inverse, basis_cat, delta, momentum, weight, replicas, flip, outs):
    _, rows, feats = delta.shape
    rank = inverse.shape[1]
    cols = momentum.shape[2]
    block = divisor(rows, 128, 16)
    steps = rows // block
    slots = min(4, steps)
    held = () if outs is None else tuple(outs)

    def body(
        place_ref, y0_ref, y1_ref, got0_ref, got1_ref, inv_ref, cat_ref, delta_ref, mom_ref, w_ref, *refs
    ):
        fb_out, mom_out, w_out, rn_out = refs[len(held) : len(held) + 4]
        rn_t, rn_cat, fb_slot, mom_slot, w_slot, sems, rn_sem = refs[len(held) + 4 :]
        slab = span(place_ref[1], cols)
        k = (place_ref[0] & 1) ^ flip
        mean = jnp.concatenate([y0_ref[...] + got0_ref[...], y1_ref[...] + got1_ref[...]], 0)
        rn_t[...] = dot_full(inv_ref[k], mean * (1.0 / replicas))
        rn_copy = pltpu.make_async_copy(rn_t, rn_out.at[k], rn_sem)
        rn_copy.start()
        hi, lo = split2(rn_t[...].T)
        rn_cat[...] = jnp.concatenate([hi, hi, lo], 1)

        def copies(i):
            at, slot = slice(i * block, (i + 1) * block), i % slots
            return [
                pltpu.make_async_copy(src.at[slot], dst.at[k, at, :], sems.at[j, slot])
                for j, (src, dst) in enumerate(
                    ((fb_slot, fb_out), (mom_slot, mom_out), (w_slot, w_out))
                )
            ]

        for i in range(steps):
            at, slot = slice(i * block, (i + 1) * block), i % slots
            if i >= slots:
                for c in copies(i - slots):
                    c.wait()
            part = rn_cat[at, :]
            fb_slot[slot] = delta_ref[k, at, :] - dot(part, cat_ref[k])
            mom = momentum_decay * mom_ref[k, at, :] + dot(part, cat_ref[k, :, slab])
            mom_slot[slot] = mom
            w_slot[slot] = (w_ref[k, at, slab].astype(f32) - step_rate * mom).astype(bf16)
            for c in copies(i):
                c.start()
        for i in range(steps - slots, steps):
            for c in copies(i):
                c.wait()
        rn_copy.wait()

    operands = (*ys, *gots, inverse, basis_cat, in_vmem(delta), momentum, weight)
    return call(
        body, place, (*operands, *held),
        [
            shape(2, rows, feats), shape(2, rows, cols),
            shape(2, rows, cols, dtype=bf16), shape(2, rank, rows),
        ],
        10, rows * feats * 256, name="finish",
        in_specs=[smem] + [vmem] * len(operands) + [hbm] * len(held),
        out_specs=[hbm] * 4,
        input_output_aliases={1 + len(operands) + i: i for i in range(len(held))},
        scratch_shapes=[
            pltpu.VMEM((rank, rows), f32),
            pltpu.VMEM((rows, 3 * rank), bf16),
            pltpu.VMEM((slots, block, feats), f32),
            pltpu.VMEM((slots, block, cols), f32),
            pltpu.VMEM((slots, block, cols), bf16),
            pltpu.SemaphoreType.DMA((3, slots)),
            pltpu.SemaphoreType.DMA,
        ],
    )


def swap(x, axis, mask):
    size = lax.axis_size(axis)
    return lax.ppermute(x, axis, [(i, i ^ mask) for i in range(size)])


def after(x, *others):
    return lax.optimization_barrier((x, *others))[0]


def has(place_ref, mask):
    return (place_ref[0] & mask) != 0


def tree(terms):
    while len(terms) > 1:
        terms = [a + b for a, b in zip(terms[::2], terms[1::2])]
    return terms[0]


def add(place, terms):
    def body(place_ref, *refs):
        refs[-1][...] = tree([r[...] for r in refs[:-1]])

    return call(body, place, terms, shape(*terms[0].shape), 4, name="add")


def add_pairs(place, ours, gots):
    count = len(ours)

    def body(place_ref, *refs):
        for j in range(count):
            refs[2 * count + j][...] = refs[j][...] + refs[count + j][...]

    out = [shape(*x.shape) for x in ours]
    return call(body, place, (*ours, *gots), out, 4, name="add_pairs")


def part_of(place_ref, mask=0):
    return (place_ref[0] ^ mask) // 2


def add_cores(place, keep, got, parts):
    rank, feats = keep.shape
    width = feats // parts

    def body(place_ref, keep_ref, got_ref, *outs):
        for m, out in enumerate(outs):
            cols = span(part_of(place_ref, 2 * m), width)
            out[...] = keep_ref[:, cols] + got_ref[:, cols]

    return call(body, place, (keep, got), [shape(rank, width)] * parts, 4, name="add_cores")


def join(place, pieces):
    rank, width = pieces[0].shape

    def body(place_ref, *refs):
        for m, piece in enumerate(refs[:-1]):
            refs[-1][:, span(part_of(place_ref, 2 * m), width)] = piece[...]

    return call(body, place, pieces, shape(rank, width * len(pieces)), 4, name="join")


def left_total(place, keep, got, work):
    fsdp, rep = lax.axis_size("fsdp"), lax.axis_size("rep")
    parts = fsdp // 2

    def beside(sends, axis, masks, i):
        got = [swap(x, axis, m) for x, m in zip(sends, masks)]
        return list(lax.optimization_barrier((*got, work(sends, i)))[:-1])

    far = range(2, fsdp, 2)
    mine, *sends = add_cores(place, keep, got, parts)
    mine = add(place, [mine] + beside(sends, "fsdp", far, 0))
    mine = add(place, [mine] + beside([mine] * (rep - 1), "rep", range(1, rep), 1))
    mine = join(place, [mine] + beside([mine] * (parts - 1), "fsdp", far, 2))
    return mine, swap(mine, "fsdp", 1)


def per_device(tokens, upstream, weight, feedback, momentum, right_factor):
    fsdp, replicas = lax.axis_size("fsdp"), lax.axis_size("rep")
    place = jnp.stack([lax.axis_index("fsdp"), lax.axis_index("rep")]).astype(jnp.int32)
    own = tokens[0]
    per, feats = own.shape
    inner = [1 << b for b in range(fsdp.bit_length() - 3)]
    far_x, far_y = fsdp // 4, fsdp // 2
    right_t = jnp.swapaxes(right_factor, 1, 2)
    scale = 1.0 / replicas

    def gather_inner(part, even_mask, odd_mask):
        parts, inners = [part], [0]
        for m in inner:
            parts = parts + [swap(p, "fsdp", m) for p in parts]
            inners = inners + [o ^ m for o in inners]
        masks = even_mask, odd_mask
        return parts, [(o ^ masks[o & 1], o ^ masks[1 - (o & 1)]) for o in inners]

    def swap_far(x, even_mask, odd_mask):
        masks = even_mask, odd_mask
        return lax.ppermute(x, "fsdp", [(i, i ^ masks[i & 1]) for i in range(fsdp)])

    grads, toks = [], []

    def forward(parts, offsets, left, last=False):
        grad, tok, left = forward_chunk(
            place, parts, offsets, weight, upstream[0], right_t, left, last
        )
        grads.append(grad)
        toks.append(tok)
        return left

    got_1 = swap_far(own, far_x, far_y)
    got_2 = swap_far(own, far_y, far_x)
    chunk_0 = gather_inner(own, 0, 0)
    delta, left_t = feedback_left(place, feedback[0], right_t)
    left_t = forward(*chunk_0, left_t)
    got_1, got_2, left_t = lax.optimization_barrier((got_1, got_2, left_t))
    got_3 = swap_far(got_1, far_y, far_x)
    chunk_1 = gather_inner(got_1, far_x, far_y)
    chunk_2 = gather_inner(got_2, far_y, far_x)
    left_t = forward(chunk_1[0] + chunk_2[0], chunk_1[1] + chunk_2[1], left_t)
    got_3, left_t = lax.optimization_barrier((got_3, left_t))
    chunk_3 = gather_inner(got_3, far_x ^ far_y, far_x ^ far_y)
    got = swap(forward(*chunk_3, left_t, last=True), "fsdp", 1)
    keep = keep_left(place, right_t, grads[-1], toks[-1], left_t)

    cuts = [0, feats // 4, 3 * feats // 4, feats]

    def work(sends, i):
        nonlocal delta
        delta = gradient(place, after(delta, *sends), grads, toks, cuts[i], cuts[i + 1])
        return delta

    mine, other = left_total(place, keep, got, work)
    masks = [(2 << b) - 1 for b in range(replicas.bit_length() - 1)]
    orders = list(zip(masks, masks[::-1]))
    last = len(orders) - 1

    def exchange(bands, step):
        return [swap(x, "rep", m) for x, m in zip(bands, orders[step])]

    y_a = project(place, delta, mine, 0, scale)
    got_a = exchange(y_a, 0)
    y_b = project(place, delta, after(other, *y_a), 1, scale)
    got_b = exchange(y_b, 0)
    *got_a, _ = lax.optimization_barrier((*got_a, y_b[0]))
    for t in range(last):
        y_a = add_pairs(place, y_a, got_a)
        got_a = exchange(y_a, t + 1)
    inverse, basis_cat = factorize(place, after(mine, *y_a), other, scale)
    *got_b, inverse = lax.optimization_barrier((*got_b, inverse))
    for t in range(last):
        y_b = add_pairs(place, y_b, got_b)
        got_b = exchange(y_b, t + 1)
    common = inverse, basis_cat, delta, momentum, weight, replicas
    *done, rn_t = finish(place, y_a, got_a, *common, 0, None)
    *got_b, rn_t = lax.optimization_barrier((*got_b, rn_t))
    feedback_next, momentum_next, weight_next, rn_t = finish(
        place, y_b, got_b, *common, 1, (*done, rn_t)
    )
    return (feedback_next[None], momentum_next, weight_next, jnp.swapaxes(rn_t, 1, 2))


def solution(mesh):
    placed = (
        P("rep", "fsdp", None),
        P("rep", "fsdp", None),
        P(None, "fsdp", None),
        P("rep", None, "fsdp", None),
        P(None, "fsdp", "rep"),
        P(None, "fsdp", None),
    )
    return jax.shard_map(
        per_device,
        mesh=mesh,
        in_specs=placed,
        out_specs=(
            P("rep", None, "fsdp", None),
            P(None, "fsdp", "rep"),
            P(None, "fsdp", "rep"),
            P(None, "fsdp", None),
        ),
        check_vma=False,
    )
```
